32 devices in a mesh: seq: 8 (over z, y), ch: 4 (over x, core).
Axes of the slice: x: 2, y: 2, z: 4, core: 2. Of those that a mesh axis runs over, the one named last changes fastest.
Arguments:
- tokens: float32 [4, 2048, 2048], P(None, 'seq'), may hold values from -6 to 6
- cotangent: float32 [4, 2048, 2048], P(None, 'seq'), may hold values from -6 to 6
- doc_starts: int32 [4, 48], replicated, may hold values from 0 to 2047, as said below
- norm1_gain: float32 [2048], replicated, may hold values from 0.5 to 1.5
- branch_gate_w: float32 [2048, 2560], P('seq', 'ch'), may hold values from -0.125 to 0.125
- branch_in_w: float32 [2048, 2560], P('seq', 'ch'), may hold values from -0.125 to 0.125
- branch_out_w: float32 [2560, 2048], P('ch', 'seq'), may hold values from -0.25 to 0.25
- conv_weight: float32 [4, 2560], P(None, 'ch'), may hold values from -3 to 3
- conv_bias: float32 [2560], P('ch'), may hold values from -3 to 3
- decay_param: float32 [2560], P('ch'), may hold values from 3 to 16
- recur_gate_w: float32 [16, 160, 160], P('ch'), may hold values from -0.5 to 0.5
- recur_gate_b: float32 [2560], P('ch'), may hold values from -4 to 4
- input_gate_w: float32 [16, 160, 160], P('ch'), may hold values from -0.5 to 0.5
- input_gate_b: float32 [2560], P('ch'), may hold values from -4 to 4
- norm2_gain: float32 [2048], replicated, may hold values from 0.5 to 1.5
- mlp_gate_w: float32 [2048, 6144], P('seq', 'ch'), may hold values from -0.125 to 0.125
- mlp_up_w: float32 [2048, 6144], P('seq', 'ch'), may hold values from -0.125 to 0.125
- mlp_down_w: float32 [6144, 2048], P('ch', 'seq'), may hold values from -0.15625 to 0.15625
Outputs:
- result: float32 [4, 2048, 2048], P(None, 'seq')
- block_states: float32 [4, 8, 2560], P(None, 'seq', 'ch')
- token_grad: float32 [4, 2048, 2048], P(None, 'seq')
- norm1_gain_grad: float32 [2048], replicated
- branch_gate_w_grad: float32 [2048, 2560], P('seq', 'ch')
- branch_in_w_grad: float32 [2048, 2560], P('seq', 'ch')
- branch_out_w_grad: float32 [2560, 2048], P('ch', 'seq')
- conv_weight_grad: float32 [4, 2560], P(None, 'ch')
- conv_bias_grad: float32 [2560], P('ch')
- decay_param_grad: float32 [2560], P('ch')
- recur_gate_w_grad: float32 [16, 160, 160], P('ch')
- recur_gate_b_grad: float32 [2560], P('ch')
- input_gate_w_grad: float32 [16, 160, 160], P('ch')
- input_gate_b_grad: float32 [2560], P('ch')
- norm2_gain_grad: float32 [2048], replicated
- mlp_gate_w_grad: float32 [2048, 6144], P('seq', 'ch')
- mlp_up_w_grad: float32 [2048, 6144], P('seq', 'ch')
- mlp_down_w_grad: float32 [6144, 2048], P('ch', 'seq')
The draws below stay inside these ranges and needn't reach their ends.
Inputs may be any that keep to these rules, and one draw needn't show every extreme that they name: `doc_starts`: each row lists 48 positions in ascending order, repeats allowed, the first 0; a document begins at every listed position.
All inputs are finite; a program needn't handle non-finite values.
Results may differ from the reference program's by a relative error of at most 0.011.
Values may be sent and summed in bfloat16 or wider, within the bound.
No kernel may reach another device: no remote copies, remote signals or barrier semaphores. Data moves between devices by JAX's collectives and lax.ppermute only.
A program may use at most 320 MiB of HBM per device.

```python
import math
import jax
import jax.numpy as jnp
from jax import lax

D = 2048
R = 2560
BLOCKS = 16
FF = 6144
SPAN = 256
ROWS = 4
DOCS = 48
BLOCK = 160
SEQ_LEN = 2048
N_SEQ = 8


def draw_doc_starts(key, part):
    key = jax.random.fold_in(key, 7)
    key_spread, key_early, key_late, key_row = jax.random.split(key, 4)
    scattered = jax.random.randint(key_spread, (ROWS, DOCS - 1), 1, SEQ_LEN)
    half_count = (DOCS - 1) // 2
    early_pos = jax.random.randint(key_early, (DOCS - 1,), 1, SPAN)
    late_pos = jax.random.randint(key_late, (DOCS - 1,), SEQ_LEN - SPAN + 1, SEQ_LEN)
    index_list = jnp.arange(DOCS - 1)
    edges = jnp.where(index_list < half_count, early_pos, late_pos)
    edges = jnp.where(index_list == DOCS - 2, SEQ_LEN - 1, edges)
    chosen = jax.random.randint(key_row, (), 0, ROWS)
    picked = jnp.arange(ROWS)[:, None] == chosen
    listed = jnp.sort(jnp.where(picked, edges[None, :], scattered), axis=1)
    return jnp.concatenate([jnp.zeros((ROWS, 1), jnp.int32), listed.astype(jnp.int32)], axis=1)


def draw_decay_param(key, part):
    key = jax.random.fold_in(key, 11)
    key_pick, key_slow, key_fast = jax.random.split(key, 3)
    slow_share = 0.5
    picked = jax.random.uniform(key_pick, (R,)) < slow_share
    slow_rate = jnp.exp(jax.random.uniform(key_slow, (R,), minval=math.log(0.2 / SEQ_LEN), maxval=math.log(1.5 / SEQ_LEN)))
    fast_rate = jnp.exp(jax.random.uniform(key_fast, (R,), minval=math.log(0.02), maxval=math.log(0.06)))
    step_rate = jnp.where(picked, slow_rate, fast_rate)
    return jnp.log(4.0 / step_rate).astype(jnp.float32)


def raised(values, own_key, source, target, parts, factor):
    owner, partner = [(jnp.arange(values.shape[axis_at]) // (values.shape[axis_at] // parts)).reshape([-1 if axis == axis_at else 1 for axis in range(values.ndim)]) for axis_at in (source, target)]
    chosen = jax.random.permutation(own_key, parts)[partner]
    strong = (owner == chosen) | (owner == (partner + parts // 2) % parts)
    return jnp.where(strong, factor * values, values)


def level_of(rng, dims, pieces, low, largest):
    factor_of = 1.0
    for position, parts in pieces:
        steps = jax.random.uniform(jax.random.fold_in(jax.random.fold_in(rng, 6), position), (parts,), jnp.float32, low / len(pieces), largest / len(pieces))
        factor_of = factor_of * jnp.repeat(jnp.exp(steps), dims[position] // parts).reshape((-1,) + (1,) * (len(dims) - 1 - position))
    return factor_of


def normal_values(rng, shape, spread, limit, shards=(), held_as=jnp.bfloat16):
    loudness = level_of(rng, shape, shards, -0.22, 0.18) if shards else 1.0
    values = jax.random.normal(rng, shape, jnp.float32) * spread * loudness
    return jnp.minimum(jnp.maximum(values, -limit), limit).astype(held_as)


def bell_draw_with(stream_key, dims, spread, limit, pieces, heavy, kind=jnp.bfloat16):
    values = spread * jax.random.normal(stream_key, dims, jnp.float32)
    if pieces:
        values = values * level_of(stream_key, dims, pieces, -0.22, 0.18)
    return jnp.clip(raised(values, jax.random.fold_in(stream_key, 3), *heavy), -limit, limit).astype(kind)


def setup_inputs(seed: int = 0) -> dict:
    seeds = jax.random.split(jax.random.key(seed), 19)
    return {
        "tokens": bell_draw_with(seeds[0], (ROWS, SEQ_LEN, D), 1.0, 6.0, ((1, 8),), (1, 2, 8, 2.0), jnp.float32),
        "cotangent": bell_draw_with(seeds[1], (ROWS, SEQ_LEN, D), 1.0, 6.0, ((1, 8),), (1, 2, 8, 2.0), jnp.float32),
        "doc_starts": draw_doc_starts(jax.random.fold_in(seeds[18], 71), 0),
        "norm1_gain": jnp.clip(1.0 + 0.1 * jax.random.normal(seeds[3], (D,), jnp.float32), 0.5, 1.5),
        "branch_gate_w": normal_values(seeds[4], (D, R), D ** -0.5, 0.125, ((0, 8), (1, 4)), jnp.float32),
        "branch_in_w": normal_values(seeds[5], (D, R), D ** -0.5, 0.125, ((0, 8), (1, 4)), jnp.float32),
        "branch_out_w": normal_values(seeds[6], (R, D), (R // 4) ** -0.5, 0.25, ((0, 4), (1, 8)), jnp.float32),
        "conv_weight": normal_values(seeds[7], (4, R), 0.5, 3.0, ((1, 4),), jnp.float32),
        "conv_bias": normal_values(seeds[8], (R,), 0.5, 3.0, ((0, 4),), jnp.float32),
        "decay_param": draw_decay_param(jax.random.fold_in(seeds[18], 71), 0),
        "recur_gate_w": normal_values(seeds[10], (BLOCKS, BLOCK, BLOCK), BLOCK ** -0.5, 0.5, ((0, 4),), jnp.float32),
        "recur_gate_b": normal_values(seeds[11], (R,), 1.0, 4.0, ((0, 4),), jnp.float32),
        "input_gate_w": normal_values(seeds[12], (BLOCKS, BLOCK, BLOCK), BLOCK ** -0.5, 0.5, ((0, 4),), jnp.float32),
        "input_gate_b": normal_values(seeds[13], (R,), 1.0, 4.0, ((0, 4),), jnp.float32),
        "norm2_gain": jnp.clip(1.0 + 0.1 * jax.random.normal(seeds[14], (D,), jnp.float32), 0.5, 1.5),
        "mlp_gate_w": normal_values(seeds[15], (D, FF), D ** -0.5, 0.125, ((0, 8), (1, 4)), jnp.float32),
        "mlp_up_w": normal_values(seeds[16], (D, FF), D ** -0.5, 0.125, ((0, 8), (1, 4)), jnp.float32),
        "mlp_down_w": normal_values(seeds[17], (FF, D), (FF // 4) ** -0.5, 0.15625, ((0, 4), (1, 8)), jnp.float32),
    }


@jax.custom_vjp
def low(v):
    return lax.optimization_barrier(v.astype(jnp.bfloat16)).astype(jnp.float32)

@jax.custom_vjp
def low_back(v):
    return v

def low_keep(v):
    return (low(v), None)

def low_pass(kept, grad):
    return (grad,)

def back_keep(v):
    return (v, None)

def back_low(kept, grad):
    return (low(grad),)
low.defvjp(low_keep, low_pass)
low_back.defvjp(back_keep, back_low)

def rms_norm(values, gain):
    return values * lax.rsqrt(lax.optimization_barrier(jnp.mean(values * values, axis=-1, keepdims=True)) + 1e-06) * gain

def tap_masks(reset_ext, length):
    blocked = reset_ext[:, 3:3 + length]
    mask_list = []
    for shift_lag in (1, 2, 3):
        mask_list.append(jnp.where(blocked, 0.0, 1.0)[..., None])
        blocked = blocked | reset_ext[:, 3 - shift_lag:3 - shift_lag + length]
    return mask_list

def gate_values(conv_values, recur_weight, recur_bias, input_weight, input_bias):
    row_count, length, channels = conv_values.shape
    grouped = conv_values.reshape(row_count, length, recur_weight.shape[0], recur_weight.shape[1])
    recur_pre = jnp.einsum('rtbi,bij->rtbj', grouped, recur_weight, precision=lax.Precision.HIGHEST).reshape(row_count, length, channels) + recur_bias
    input_pre = jnp.einsum('rtbi,bij->rtbj', grouped, input_weight, precision=lax.Precision.HIGHEST).reshape(row_count, length, channels) + input_bias
    return (jax.nn.sigmoid(recur_pre), jax.nn.sigmoid(input_pre))

def decay_terms(recur_gate, param, reset_here):
    log_decay = -8.0 * jax.nn.softplus(-param) * recur_gate
    decay_rate = jnp.where(reset_here[..., None], 0.0, jnp.exp(log_decay))
    factor = jnp.where(reset_here[..., None], 1.0, jnp.sqrt(-jnp.expm1(2.0 * log_decay)))
    return (decay_rate, factor)

def affine(earlier, later):
    return (earlier[0] * later[0], later[0] * earlier[1] + later[1])

def dense(left, right):
    return jnp.einsum('rtd,df->rtf', left, right, precision=lax.Precision.HIGHEST)

def reference(tokens, cotangent, doc_starts, norm1_gain, branch_gate_w, branch_in_w, branch_out_w, conv_weight, conv_bias, decay_param, recur_gate_w, recur_gate_b, input_gate_w, input_gate_b, norm2_gain, mlp_gate_w, mlp_up_w, mlp_down_w):
    seq_len = SPAN * N_SEQ
    positions = jnp.arange(seq_len, dtype=jnp.int32)
    reset_here = jnp.any(doc_starts[:, :, None] == positions[None, None, :], axis=1)
    reset_ext = jnp.pad(reset_here, ((0, 0), (3, 0)))
    valid_list = tap_masks(reset_ext, seq_len)

    def forward(tokens, norm1_gain, branch_gate_w, branch_in_w, branch_out_w, conv_weight, conv_bias, decay_param, recur_gate_w, recur_gate_b, input_gate_w, input_gate_b, norm2_gain, mlp_gate_w, mlp_up_w, mlp_down_w):
        hidden_one = low(rms_norm(tokens, norm1_gain))
        pre_gate = low_back(dense(hidden_one, low(branch_gate_w)))
        pre_input = low_back(dense(hidden_one, low(branch_in_w)))
        gate_act = jax.nn.gelu(pre_gate)
        padded = jnp.pad(pre_input, ((0, 0), (3, 0), (0, 0)))
        conv_out = conv_bias + conv_weight[0] * pre_input
        for shift_lag in (1, 2, 3):
            conv_out = conv_out + conv_weight[shift_lag] * padded[:, 3 - shift_lag:3 - shift_lag + seq_len] * valid_list[shift_lag - 1]
        recur_gate, input_gate = gate_values(conv_out, recur_gate_w, recur_gate_b, input_gate_w, input_gate_b)
        decay_rate, factor = decay_terms(recur_gate, decay_param, reset_here)
        driven = factor * input_gate * conv_out
        unused_decay, rec_state = lax.associative_scan(affine, (decay_rate, driven), axis=1)
        mixed_val = low(gate_act * rec_state)
        after_one = tokens + low_back(dense(mixed_val, low(branch_out_w)))
        hidden_two = low(rms_norm(after_one, norm2_gain))
        pre_mlp = low_back(dense(hidden_two, low(mlp_gate_w)))
        pre_up = low_back(dense(hidden_two, low(mlp_up_w)))
        product = low(jax.nn.gelu(pre_mlp) * pre_up)
        result = after_one + low_back(dense(product, low(mlp_down_w)))
        return (result, rec_state)
    (result, rec_state), backward = jax.vjp(forward, tokens, norm1_gain, branch_gate_w, branch_in_w, branch_out_w, conv_weight, conv_bias, decay_param, recur_gate_w, recur_gate_b, input_gate_w, input_gate_b, norm2_gain, mlp_gate_w, mlp_up_w, mlp_down_w)
    grads = backward((cotangent, jnp.zeros_like(rec_state)))
    block_states = rec_state[:, SPAN - 1::SPAN]
    return (result, block_states, grads[0], grads[1], grads[2], grads[3], grads[4], grads[5], grads[6], grads[7], grads[8], grads[9], grads[10], grads[11], grads[12], grads[13], grads[14], grads[15])
```

```python
import jax
import jax.numpy as jnp
from jax import lax
from jax.experimental import pallas as pl
from jax.experimental.pallas import tpu as pltpu
from jax.sharding import PartitionSpec as P

LOW = jnp.bfloat16
F32 = jnp.float32
EPS = 1e-06
GELU_A = 0.7978845608028654
GELU_B = 0.044715
VMEM_LIMIT = 48 * 1024 * 1024
RING_LIMIT = 8
WINDOW = 256
SMALL_COST = pl.CostEstimate(flops=1, bytes_accessed=1, transcendentals=0)


def ring_order(count):
    return list(range(0, count, 2)) + list(range(count - 1, 0, -2))


def ring_place(seq_index, count):
    return jnp.where(seq_index % 2 == 0, seq_index // 2, count - 1 - seq_index // 2)


def ring_member(place, count):
    place = place % count
    return jnp.where(place < count // 2, 2 * place, 2 * (count - 1 - place) + 1)


def ring_pairs(count):
    order = ring_order(count)
    ahead = [(order[i], order[(i + 1) % count]) for i in range(count)]
    behind = [(target, source) for source, target in ahead]
    return ahead, behind


def ring_blocks(count):
    if count > RING_LIMIT:
        return [jnp.int32(0)]
    here = ring_place(lax.axis_index("seq"), count)
    offsets = [0]
    for step in range(1, count // 2):
        offsets += [-step, step]
    return [ring_member(here + offset, count) for offset in offsets + [count // 2]]


def ring_block(offset, count):
    if abs(offset) == count // 2:
        return count - 1
    return 2 * offset if offset >= 0 else -2 * offset - 1


def after_that(value, others):
    return lax.optimization_barrier((value, others))[0]


def meet(value, *rings):
    value, pieces = lax.optimization_barrier((value, [ring.latest for ring in rings]))
    for ring, came in zip(rings, pieces, strict=True):
        ring.replace(came)
    return value


class Gather:
    def __init__(self, shards, others=()):
        self.count = lax.axis_size("seq")
        self.shards = shards
        joined = jnp.concatenate(shards, axis=1) if len(shards) > 1 else shards[0]
        self.latest, self.others = (joined, joined), others
        self.up, self.down = [self.latest[0]], [self.latest[1]]

    def replace(self, pieces):
        self.latest = pieces
        if self.count <= RING_LIMIT:
            self.up[-1], self.down[-1] = pieces

    def step(self):
        if self.count <= RING_LIMIT and len(self.up) <= self.count // 2:
            ahead, behind = ring_pairs(self.count)
            cut = self.shards[0].shape[0] // 2
            first, second = self.latest
            if len(self.up) == self.count // 2:
                first, second = first[:cut], second[cut:]
            first, second = after_that((first, second), self.others)
            self.others = ()
            self.up.append(lax.ppermute(first, "seq", ahead))
            self.down.append(lax.ppermute(second, "seq", behind))
            self.latest = (self.up[-1], self.down[-1])
        return self.latest

    def full(self):
        if self.count > RING_LIMIT:
            return [lax.all_gather(shard, "seq", axis=0, tiled=True) for shard in self.shards]
        pieces = [self.up[0]]
        for first, second in zip(self.up[1:], self.down[1:], strict=True):
            pieces += [first, second]
        full, start = [], 0
        for shard in self.shards:
            stop = start + shard.shape[1]
            full.append(jnp.concatenate([piece[:, start:stop] for piece in pieces], axis=0))
            start = stop
        return full


class Reduce:
    def __init__(self, fulls, others=()):
        self.count = lax.axis_size("seq")
        self.fulls = fulls
        self.left = self.count // 2
        self.latest, self.sent = (), ()
        self.others = others

    def replace(self, pieces):
        self.latest = pieces

    def step(self):
        if self.count <= RING_LIMIT and self.left > 0:
            ahead, behind = ring_pairs(self.count)
            up, down = ring_step(self.fulls, self.latest, self.count, self.left)
            up, down = after_that((up, down), self.others)
            self.others = ()
            self.sent = (up, down)
            self.latest = (lax.ppermute(up, "seq", ahead), lax.ppermute(down, "seq", behind))
            self.left -= 1
        return self.sent

    def sums(self):
        if self.count > RING_LIMIT:
            return [
                lax.psum_scatter(full.astype(F32), "seq", scatter_dimension=0, tiled=True)
                for full in self.fulls
            ]
        return ring_step(self.fulls, self.latest, self.count, 0)


def ring_step(fulls, came, count, step):
    half, rows = count // 2, fulls[0].shape[0] // count
    widths = [full.shape[1] for full in fulls]
    total = sum(widths)
    parts = 4
    piece = rows // parts
    first, last = step == half, step == 0

    def kernel(*refs):
        ups, downs = refs[: len(fulls)], refs[len(fulls) : 2 * len(fulls)]
        rest = refs[2 * len(fulls) :]
        got, out = rest[: len(came)], rest[len(came) :]
        place = pl.program_id(0)
        start = 0
        for index, width in enumerate(widths):
            columns = slice(start, start + width)
            start += width
            up, down = ups[index][...].astype(F32), downs[index][...].astype(F32)
            if last:
                out[index][...] = up + got[0][:, columns].astype(F32) + got[1][:, columns].astype(F32)
                continue
            if not first:
                plus, minus = got[0][:, columns].astype(F32), got[1][:, columns].astype(F32)
                if step == half - 1:
                    plus = jnp.where(place < parts // 2, plus, 0.0)
                    minus = jnp.where(place >= parts // 2, minus, 0.0)
                up, down = up + plus, down + minus
            out[0][:, columns] = up.astype(LOW)
            out[1][:, columns] = down.astype(LOW)

    def at(place, offset=0):
        block = ring_block(place, count)
        return lambda i: (block * parts + i + offset, 0)

    grid = parts // 2 if first else parts
    blocks = [pl.BlockSpec((piece, w), at(step)) for w in widths]
    blocks += [pl.BlockSpec((piece, w), at(-step, parts // 2 if first else 0)) for w in widths]
    got_specs = [pl.BlockSpec((piece, total), lambda i: (i, 0))] * len(came)
    if step == half - 1:
        got_specs = [
            pl.BlockSpec((piece, total), lambda i: (jnp.minimum(i, parts // 2 - 1), 0)),
            pl.BlockSpec((piece, total), lambda i: (jnp.maximum(i - parts // 2, 0), 0)),
        ]
    if last:
        out_specs = [pl.BlockSpec((piece, w), lambda i: (i, 0)) for w in widths]
        out_shape = [shape_of((rows, w)) for w in widths]
    else:
        out_specs = [pl.BlockSpec((piece, total), lambda i: (i, 0))] * 2
        out_shape = [shape_of((grid * piece, total), LOW)] * 2
    return pl.pallas_call(
        kernel, grid=(grid,), in_specs=blocks + got_specs, out_specs=out_specs,
        out_shape=out_shape, compiler_params=params(), cost_estimate=SMALL_COST, name="ring_step",
    )(*fulls, *fulls, *came)


ROW_ORDER = (0, 2, 1, 3)


def near_pairs(count):
    return [(c, c ^ 1) for c in range(count)]


def far_pairs(count):
    return [(c, c ^ 2) for c in range(count)]


def to_near(value):
    return lax.ppermute(value, "ch", near_pairs(lax.axis_size("ch")))


def to_far(value):
    return lax.ppermute(value, "ch", far_pairs(lax.axis_size("ch")))


def spread_rows(own):
    far, near = to_far(own), to_near(own)
    return [own, far, near, to_near(far)]


def sum_over(value, axis, dtype=F32):
    count, step = lax.axis_size(axis), 1
    while step < count:
        sent = value.astype(dtype)
        came = lax.ppermute(sent, axis, [(c, c ^ step) for c in range(count)])
        value = sent.astype(F32) + came.astype(F32)
        step *= 2
    return value


def carried(ends, backward):
    count, mine = lax.axis_size("seq"), lax.axis_index("seq")
    pieces = to_all(ends[:, :2].reshape(-1, ends.shape[2]), "seq").reshape(
        count, ends.shape[0], 2, ends.shape[2]
    )
    total = jnp.zeros_like(ends[:, 0])
    for place in range(count - 1):
        member = count - 1 - place if backward else place
        counts = member > mine if backward else member < mine
        piece = pieces[member]
        total = jnp.where(counts, piece[:, 0] * total + piece[:, 1], total)
    return total


def to_all(value, axis):
    count = lax.axis_size(axis)
    return lax.all_to_all(
        jnp.broadcast_to(value[None], (count,) + value.shape), axis, 0, 0, tiled=True
    )


def row_block(shape, column=0):
    return pl.BlockSpec((1,) + shape, lambda row, *_: (row, 0, column))


def whole_block(shape):
    return pl.BlockSpec(shape, lambda row, *_: (0,) * len(shape))


def gelu_parts(value):
    tanh = jnp.tanh(GELU_A * (value + GELU_B * value * value * value))
    act = 0.5 * value * (1.0 + tanh)
    slope = 0.5 * (1.0 + tanh) + 0.5 * value * (1.0 - tanh * tanh) * GELU_A * (
        1.0 + 3.0 * GELU_B * value * value
    )
    return act, slope


def gelu(value):
    return gelu_parts(value)[0]


def minus_expm1(value):
    series = jnp.full_like(value, 1.0 / 11.0)
    for divisor in range(10, 1, -1):
        series = (1.0 + value * series) * (1.0 / divisor)
    series = -value * (1.0 + value * series)
    return jnp.where(value > -0.8, series, 1.0 - jnp.exp(value))


def split(value):
    high = value.astype(LOW)
    return high, (value - high.astype(F32)).astype(LOW)


def dot(left, right, contract):
    return lax.dot_general(left, right, (contract, ((), ())), preferred_element_type=F32)


def dot_three(left, right, contract):
    (left_high, left_low), (right_high, right_low) = left, right
    return (
        dot(left_high, right_high, contract)
        + dot(left_high, right_low, contract)
        + dot(left_low, right_high, contract)
    )


def windows(count, size):
    starts = [min(block * size // 128 * 128, count * size - WINDOW) for block in range(count)]
    return [(start, block * size - start) for block, start in enumerate(starts)]


def window_dots(value, high_ref, low_ref, first, spots, contract):
    parts = []
    for index, (start, _) in enumerate(spots):
        piece = split(value[:, start : start + WINDOW])
        weight = (high_ref[first + index], low_ref[first + index])
        parts.append((start, dot_three(piece, weight, contract)))
    columns = []
    for tile in range(0, value.shape[1], 128):
        total = None
        for start, part in parts:
            if start <= tile < start + WINDOW:
                share = part[:, tile - start : tile - start + 128]
                total = share if total is None else total + share
        columns.append(total)
    return jnp.concatenate(columns, axis=1)


def decay_and_factor(recur, coef, reset):
    log_decay = coef * recur
    plain = jnp.exp(log_decay)
    decay = jnp.where(reset, 0.0, plain)
    factor = jnp.where(reset, 1.0, jnp.sqrt(minus_expm1(2.0 * log_decay)))
    return plain, decay, factor


def tile_scan(alpha, beta, backward):
    place = lax.broadcasted_iota(jnp.int32, alpha.shape, 1)
    for step in (1, 2, 4):
        turn = 8 - step if backward else step
        inside = place < 8 - step if backward else place >= step
        other_alpha = pltpu.roll(alpha, turn, 1)
        other_beta = pltpu.roll(beta, turn, 1)
        beta = jnp.where(inside, alpha * other_beta + beta, beta)
        alpha = jnp.where(inside, alpha * other_alpha, alpha)
    return alpha, beta


def join_tiles(alpha_ref, beta_ref, backward):
    length, channels = alpha_ref.shape[1], alpha_ref.shape[2]
    groups = length // 8

    def step(index, carry):
        alpha_carry, beta_carry = carry
        group = groups - 1 - index if backward else index
        rows = pl.ds(pl.multiple_of(group * 8, 8), 8)
        alpha, beta = alpha_ref[0, rows, :], beta_ref[0, rows, :]
        beta = alpha * beta_carry + beta
        alpha = alpha * alpha_carry
        alpha_ref[0, rows, :] = alpha
        beta_ref[0, rows, :] = beta
        last = 0 if backward else 7
        return alpha[last : last + 1], beta[last : last + 1]

    start = (jnp.ones((1, channels), F32), jnp.zeros((1, channels), F32))
    return lax.fori_loop(0, groups, step, start, unroll=4)


def forward_kernel(
    input_ref, halo_ref, mask_ref, taps_ref, bias_ref, coef_ref, high_ref, low_ref, gate_bias_ref,
    conv_ref, recur_ref, gate_ref, alpha_ref, beta_ref, export_ref, extended,
):
    length, channels = input_ref.shape[1], input_ref.shape[2]
    extended[0:8, :] = halo_ref[0]
    extended[8 : 8 + length, :] = input_ref[0]
    masks = mask_ref[0]
    conv = bias_ref[...] + taps_ref[0:1, :] * input_ref[0]
    for lag in (1, 2, 3):
        lagged = extended[8 - lag : 8 - lag + length, :]
        conv = conv + taps_ref[lag : lag + 1, :] * lagged * masks[:, lag : lag + 1]
    conv_ref[0] = conv
    count = high_ref.shape[0] // 2
    spots = windows(count, channels // count)
    before = [
        window_dots(conv, high_ref, low_ref, first, spots, ((1,), (0,))) for first in (0, count)
    ]
    recur = jax.nn.sigmoid(before[0] + gate_bias_ref[:, :channels])
    gate = jax.nn.sigmoid(before[1] + gate_bias_ref[:, channels:])
    recur_ref[0] = recur
    gate_ref[0] = gate
    reset = masks[:, 0:1] > 0.5
    _, decay, factor = decay_and_factor(recur, coef_ref[...], reset)
    driven = factor * gate * conv
    grouped = (length // 8, 8, channels)
    alpha, beta = tile_scan(decay.reshape(grouped), driven.reshape(grouped), False)
    alpha_ref[0] = alpha.reshape(length, channels)
    beta_ref[0] = beta.reshape(length, channels)
    alpha, beta = join_tiles(alpha_ref, beta_ref, False)
    export_ref[0] = jnp.concatenate([alpha, beta, jnp.zeros((6, channels), F32)], axis=0)


def backscan_kernel(
    mixed_ref, pre_ref, state_ref, recur_ref, mask_ref, coef_ref,
    pre_grad_ref, alpha_ref, beta_ref, export_ref, extended,
):
    length, channels = mixed_ref.shape[1], mixed_ref.shape[2]
    act, slope = gelu_parts(pre_ref[0])
    mixed = mixed_ref[0]
    pre_grad_ref[0] = (mixed * state_ref[0] * slope).astype(LOW)
    reset = mask_ref[0][:, 0:1] > 0.5
    decay = jnp.where(reset, 0.0, jnp.exp(coef_ref[...] * recur_ref[0]))
    extended[0:length, :] = decay
    extended[length : length + 8, :] = jnp.ones((8, channels), F32)
    following = extended[1 : 1 + length, :]
    grouped = (length // 8, 8, channels)
    alpha, beta = tile_scan(following.reshape(grouped), (mixed * act).reshape(grouped), True)
    alpha_ref[0] = alpha.reshape(length, channels)
    beta_ref[0] = beta.reshape(length, channels)
    alpha, beta = join_tiles(alpha_ref, beta_ref, True)
    first = extended[0:1, :]
    export_ref[0] = jnp.concatenate(
        [first * alpha, first * beta, jnp.zeros((6, channels), F32)], axis=0
    )


def backward_kernel(
    alpha_ref, beta_ref, incoming_ref, state_ref, carry_ref, recur_ref, gate_ref, conv_ref,
    input_ref, halo_ref, mask_ref, taps_ref, coef_ref, high_ref, low_ref, pre_grad_ref,
    grad_ref, tail_ref, head_ref, weight_ref, sums_ref, extended, masked, weight_acc,
):
    length, channels = alpha_ref.shape[1], alpha_ref.shape[2]

    @pl.when(pl.program_id(0) == 0)
    def _():
        weight_acc[...] = jnp.zeros_like(weight_acc)
        sums_ref[...] = jnp.zeros_like(sums_ref)

    masks = mask_ref[0]
    reset = masks[:, 0:1] > 0.5
    recur, gate, conv, coef = recur_ref[0], gate_ref[0], conv_ref[0], coef_ref[...]
    plain, decay, factor = decay_and_factor(recur, coef, reset)
    grad = beta_ref[0] + alpha_ref[0] * incoming_ref[0]
    extended[0:8, :] = jnp.broadcast_to(carry_ref[0], (8, channels))
    extended[8 : 8 + length, :] = state_ref[0]
    prior = extended[7 : 7 + length, :]
    grad_decay = grad * prior
    grad_factor = grad * gate * conv
    grad_log = jnp.where(reset, 0.0, grad_decay * decay - grad_factor * plain * plain / factor)
    grad_recur = coef * grad_log * recur * (1.0 - recur)
    grad_gate = grad * factor * conv * gate * (1.0 - gate)
    count = high_ref.shape[0] // 2
    size = channels // count
    spots = windows(count, size)
    grad_conv = grad * factor * gate
    for first, values in ((0, grad_recur), (count, grad_gate)):
        for index, (start, _) in enumerate(spots):
            columns = slice(start, start + WINDOW)
            pair = split(conv[:, columns]), split(values[:, columns])
            weight_acc[first + index] += dot_three(*pair, ((0,), (0,)))
        grad_conv = grad_conv + window_dots(
            values, high_ref, low_ref, first, spots, ((1,), (1,))
        )

    @pl.when(pl.program_id(0) == pl.num_programs(0) - 1)
    def _():
        for index in range(2 * count):
            place = spots[index % count][1]
            turned = weight_acc[index]
            if place:
                turned = pltpu.roll(turned, WINDOW - place, 1)
            weight_ref[index] = turned[place : place + size].astype(LOW)


    def total(value):
        return jnp.sum(value, axis=0, keepdims=True)

    extended[0:8, :] = halo_ref[0]
    extended[8 : 8 + length, :] = input_ref[0]
    sums = [total(grad_conv), total(grad_conv * input_ref[0])]
    masked[0:8, :] = jnp.zeros((8, channels), F32)
    masked[8 + length : 16 + length, :] = jnp.zeros((8, channels), F32)
    spread = taps_ref[0:1, :] * grad_conv
    head = jnp.zeros((8, channels), F32)
    for lag in (1, 2, 3):
        kept = grad_conv * masks[:, lag : lag + 1]
        sums.append(total(kept * extended[8 - lag : 8 - lag + length, :]))
        masked[8 : 8 + length, :] = kept
        tap = taps_ref[lag : lag + 1, :]
        spread = spread + tap * masked[8 + lag : 8 + lag + length, :]
        head = head + tap * masked[lag : 8 + lag, :]
    sums += [total(recur * grad_log), total(grad_recur), total(grad_gate)]
    sums_ref[...] += jnp.concatenate(sums, axis=0)
    grad_ref[0, :, :channels] = spread.astype(LOW)
    grad_ref[0, :, channels:] = pre_grad_ref[0]
    tail_ref[0] = spread[length - 8 :, :]
    head_ref[0] = head


def params():
    return pltpu.CompilerParams(
        dimension_semantics=("arbitrary",), vmem_limit_bytes=VMEM_LIMIT
    )


def shape_of(shape, dtype=F32):
    return jax.ShapeDtypeStruct(shape, dtype)


def run_forward(pre, halo, masks, taps, bias, coef, high, low, gate_bias):
    rows, length, channels = pre.shape[0], pre.shape[1], taps.shape[1]
    block = row_block((length, channels))
    return pl.pallas_call(
        forward_kernel,
        grid=(rows,),
        in_specs=[
            block, row_block((8, channels)), row_block((length, 8)), whole_block((4, channels)),
            whole_block((1, channels)), whole_block((1, channels)), whole_block(high.shape),
            whole_block(low.shape), whole_block((1, 2 * channels)),
        ],
        out_specs=[block] * 5 + [row_block((8, channels))],
        out_shape=[shape_of((rows, length, channels))] * 5 + [shape_of((rows, 8, channels))],
        scratch_shapes=[pltpu.VMEM((length + 8, channels), F32)],
        compiler_params=params(), cost_estimate=SMALL_COST,
        name="forward_scan",
    )(pre, halo, masks, taps, bias, coef, high, low, gate_bias)


def run_backscan(mixed, pre, state, recur, masks, coef):
    rows, length, channels = mixed.shape
    block = row_block((length, channels))
    return pl.pallas_call(
        backscan_kernel,
        grid=(rows,),
        in_specs=[
            block, row_block((length, channels), 1), block, block, row_block((length, 8)),
            whole_block((1, channels)),
        ],
        out_specs=[block] * 3 + [row_block((8, channels))],
        out_shape=[
            shape_of(mixed.shape, LOW), shape_of(mixed.shape), shape_of(mixed.shape),
            shape_of((rows, 8, channels)),
        ],
        scratch_shapes=[pltpu.VMEM((length + 8, channels), F32)],
        compiler_params=params(), cost_estimate=SMALL_COST,
        name="backward_scan",
    )(mixed, pre, state, recur, masks, coef)


def run_backward(
    alpha, beta, incoming, state, carry, recur, gate, conv, pre, halo, masks, taps, coef, high, low, pre_grad
):
    rows, length, channels = alpha.shape
    block, edge, line = (
        row_block((length, channels)), row_block((8, channels)), row_block((1, channels)),
    )
    weights = (high.shape[0], 2 * channels // high.shape[0], WINDOW)
    return pl.pallas_call(
        backward_kernel,
        grid=(rows,),
        in_specs=[
            block, block, line, block, line, block, block, block, block, edge,
            row_block((length, 8)), whole_block((4, channels)), whole_block((1, channels)),
            whole_block(high.shape), whole_block(low.shape), block,
        ],
        out_specs=[row_block((length, 2 * channels)), edge, edge, whole_block(weights), whole_block((8, channels))],
        out_shape=[
            shape_of((rows, length, 2 * channels), LOW), shape_of((rows, 8, channels)),
            shape_of((rows, 8, channels)), shape_of(weights, LOW), shape_of((8, channels)),
        ],
        scratch_shapes=[
            pltpu.VMEM((length + 8, channels), F32), pltpu.VMEM((length + 16, channels), F32),
            pltpu.VMEM(high.shape, F32),
        ],
        compiler_params=params(), cost_estimate=SMALL_COST,
        name="branch_backward",
    )(alpha, beta, incoming, state, carry, recur, gate, conv, pre, halo, masks, taps, coef, high, low, pre_grad)


def back_project(lefts, rights):
    rows, length, _ = lefts[0].shape
    width, tile = rights[0].shape[0], 256
    half = rows // 2

    def kernel(*refs):
        total = None
        for left, right in zip(refs[: len(lefts)], refs[len(lefts) : 2 * len(lefts)], strict=True):
            flat = left[...].reshape(rows * length, left.shape[2])
            share = dot(flat, right[...], ((1,), (1,)))
            total = share if total is None else total + share
        total = total.reshape(rows, length, tile)
        refs[-2][...] = total[:half]
        refs[-1][...] = total[half:].astype(LOW)

    out = pl.BlockSpec((half, length, tile), lambda i: (0, 0, i))
    in_specs = [pl.BlockSpec(left.shape, lambda i: (0, 0, 0)) for left in lefts]
    in_specs += [pl.BlockSpec((tile, right.shape[1]), lambda i: (i, 0)) for right in rights]
    return pl.pallas_call(
        kernel, grid=(width // tile,), in_specs=in_specs, out_specs=[out, out],
        out_shape=[shape_of((half, length, width)), shape_of((half, length, width), LOW)],
        compiler_params=params(), cost_estimate=SMALL_COST, name="back_project",
    )(*lefts, *rights)


def joined(kept, came):
    total = kept + came.astype(F32)
    return total[0:1], total[1:2].astype(LOW)


def part(index, width):
    return pl.ds(pl.multiple_of(index * width, 128), width)


def norm_kernel(row_map, block_map, gain_ref, values_ref, out_ref):
    blocks = block_map.shape[0]
    width = values_ref.shape[2] // blocks
    values = values_ref[0]
    root = lax.rsqrt(jnp.mean(values * values, axis=-1, keepdims=True) + EPS)
    for place in range(blocks):
        there = part(block_map[place], width)
        normed = values_ref[0, :, there] * root * gain_ref[:, there]
        out_ref[0, :, place * width : (place + 1) * width] = normed.astype(LOW)


def relative_kernel(row_map, block_map, values_ref, own_ref, *out_refs):
    blocks = block_map.shape[0]
    width = values_ref.shape[2] // blocks
    for place in range(blocks):
        there = part(block_map[place], width)
        here = slice(place * width, (place + 1) * width)
        for out_ref in out_refs:
            out_ref[0, :, here] = values_ref[0, :, there].astype(LOW)

        @pl.when(pl.program_id(0) == 0)
        def _():
            own_ref[0, :, here] = values_ref[0, :, there]


def assemble_kernel(row_map, block_map, base_ref, *refs):
    pieces, out_ref = refs[:-1], refs[-1]
    blocks = block_map.shape[0]
    width = base_ref.shape[2] // blocks
    for row, piece in enumerate(pieces):

        @pl.when(pl.program_id(0) == row)
        def _():
            for place in range(blocks):
                there = part(block_map[place], width)
                here = slice(place * width, (place + 1) * width)
                out_ref[0, :, there] = base_ref[0, :, there] + piece[0, :, here].astype(F32)


def arranged(kernel, maps, out_shape, in_specs, out_specs, *arrays):
    return pl.pallas_call(
        kernel,
        grid_spec=pltpu.PrefetchScalarGridSpec(
            num_scalar_prefetch=2, grid=(maps[0].shape[0],), in_specs=in_specs, out_specs=out_specs
        ),
        out_shape=out_shape,
        compiler_params=params(), cost_estimate=SMALL_COST,
    )(*maps, *arrays)


def mapped_row(shape):
    return pl.BlockSpec((1,) + shape, lambda row, row_map, block_map: (row_map[row], 0, 0))


def relative_norm(values, gain, maps):
    shape = values.shape[1:]
    return arranged(
        norm_kernel, maps, shape_of(values.shape, LOW),
        [whole_block((1, shape[1])), mapped_row(shape)], row_block(shape), gain[None, :], values,
    )


def relative_rows(values, maps, rounded):
    shape = values.shape[1:]
    shapes, specs = [shape_of((1,) + shape)], [whole_block((1,) + shape)]
    if rounded:
        shapes, specs = shapes + [shape_of(values.shape, LOW)], specs + [row_block(shape)]
    if not rounded:
        maps = (maps[0][:1], maps[1])
    return arranged(relative_kernel, maps, shapes, [mapped_row(shape)], specs, values)


def assemble(base, pieces, maps):
    shape = base.shape[1:]
    return arranged(
        assemble_kernel, maps, shape_of(base.shape),
        [mapped_row(shape)] + [whole_block((1,) + shape)] * len(pieces), mapped_row(shape),
        base, *pieces,
    )


def project(left, right):
    return jnp.einsum("rtd,df->rtf", left, right, preferred_element_type=F32)


def project_back(left, right):
    return jnp.einsum("rtf,df->rtd", left, right, preferred_element_type=F32)


def outer_sum(left, right):
    return jnp.einsum("rtd,rtf->df", left, right, preferred_element_type=F32).astype(LOW)


def inverse_root(values):
    return lax.rsqrt(jnp.mean(values * values, axis=-1, keepdims=True) + EPS)


def norm_back(grad, values, root, gain):
    scaled = grad * gain
    inner = jnp.mean(scaled * values, axis=-1, keepdims=True)
    share = jnp.sum(grad * values * root, axis=(0, 1))
    return root * scaled - values * (root * root * root) * inner, share


def gate_matrix_kernel(recur_ref, input_ref, high_ref, low_ref):
    count, size = recur_ref.shape[0], recur_ref.shape[1]
    high_ref[...] = jnp.zeros_like(high_ref)
    low_ref[...] = jnp.zeros_like(low_ref)
    for index, ref in enumerate((recur_ref, input_ref)):
        for block, (_, place) in enumerate(windows(count, size)):
            high, low = split(ref[block])
            here = slice(place, place + size)
            high_ref[index * count + block, here, here] = high
            low_ref[index * count + block, here, here] = low


def gate_matrix(recur_weight, input_weight):
    shape = shape_of((2 * recur_weight.shape[0], WINDOW, WINDOW), LOW)
    return pl.pallas_call(
        gate_matrix_kernel, out_shape=[shape, shape],
        compiler_params=pltpu.CompilerParams(vmem_limit_bytes=VMEM_LIMIT), cost_estimate=SMALL_COST, name="gate_matrix",
    )(recur_weight, input_weight)


def body(
    tokens, cotangent, doc_starts, norm1_gain, branch_gate_w, branch_in_w, branch_out_w,
    conv_weight, conv_bias, decay_param, recur_gate_w, recur_gate_b, input_gate_w, input_gate_b,
    norm2_gain, mlp_gate_w, mlp_up_w, mlp_down_w,
):
    rows, length, width = tokens.shape
    channels, blocks = conv_bias.shape[0], recur_gate_w.shape[0]
    seq_count = lax.axis_size("seq")
    mine, turn = lax.axis_index("seq"), lax.axis_index("ch")
    row_map = jnp.stack([turn ^ row for row in ROW_ORDER]).astype(jnp.int32)
    block_map = jnp.stack(ring_blocks(seq_count)).astype(jnp.int32)
    maps = (row_map, block_map)

    def row_of(values, row):
        return lax.dynamic_slice_in_dim(values, turn ^ ROW_ORDER[row], 1, axis=0)

    def features(values):
        return jnp.take(values.reshape(block_map.shape[0], -1), block_map, axis=0).reshape(-1)

    def features_back(values):
        there = jnp.argmax(block_map[None, :] == jnp.arange(block_map.shape[0])[:, None], axis=1)
        return jnp.take(values.reshape(block_map.shape[0], -1), there, axis=0).reshape(-1)

    gather_one = Gather(
        [
            jnp.concatenate([branch_in_w.astype(LOW), branch_gate_w.astype(LOW)], axis=1),
            branch_out_w.astype(LOW).T,
        ]
    )
    came = gather_one.step()

    starts = jnp.concatenate([row_of(doc_starts, j) for j in range(rows)], axis=0)
    positions = mine * length - 3 + jnp.arange(length + 3, dtype=jnp.int32)
    reset_ext = jnp.any(starts[:, :, None] == positions[None, None, :], axis=1)
    blocked = reset_ext[:, 3:]
    columns = [blocked.astype(F32)]
    for lag in (1, 2, 3):
        columns.append(jnp.where(blocked, 0.0, 1.0))
        blocked = blocked | reset_ext[:, 3 - lag : 3 - lag + length]
    masks = jnp.stack(columns + [jnp.zeros_like(columns[0])] * 4, axis=-1)

    gate_bias = jnp.concatenate([recur_gate_b, input_gate_b])[None, :]
    coef = (-8.0 * jax.nn.softplus(-decay_param))[None, :]
    gain_one, gain_two = features(norm1_gain), features(norm2_gain)
    mlp_shards = [mlp_gate_w.astype(LOW), mlp_up_w.astype(LOW)]
    down_shards = [mlp_down_w.astype(LOW).T]

    before = after_that(tokens[:, -8:, :], came)
    before = lax.ppermute(before, "seq", [(s, s + 1) for s in range(seq_count - 1)])
    first_maps = after_that(maps, (came, masks))
    came = gather_one.step()
    hidden_one = relative_norm(tokens, norm1_gain, first_maps)
    hidden_before = relative_norm(before, norm1_gain, first_maps)
    recur_weights = after_that(recur_gate_w, (came, hidden_before))
    came = gather_one.step()
    high, low = gate_matrix(recur_weights, input_gate_w)
    gather_two = Gather(mlp_shards, gather_one.step())
    gather_two.step()
    in_gate, output_full = gather_one.full()

    pre = project(hidden_one, in_gate)
    halo = project(hidden_before, in_gate)
    conv, recur, gate, decay_sum, state_part, export = run_forward(
        pre, halo, masks, conv_weight, conv_bias[None, :], coef, high, low, gate_bias
    )
    export = meet(export, gather_two)
    carry = carried(export, False)[:, None, :]
    came = gather_two.step()
    state = state_part + decay_sum * carry
    mixed = (gelu(pre[:, :, channels:]) * state).astype(LOW)

    kept, away = back_project([mixed], [output_full])
    kept, beyond = joined(kept, to_near(away))
    arrived = to_far(beyond)
    late_maps = after_that(maps, beyond)
    (tokens_own,) = relative_rows(tokens, late_maps, False)
    cotangent_own, grad_two = relative_rows(cotangent, late_maps, True)
    kept = meet(after_that(kept, (tokens_own, cotangent_own)), gather_two)
    after = tokens_own + (kept + arrived.astype(F32))
    came = gather_two.step()
    root_two = inverse_root(after)
    spread = spread_rows((after * root_two * gain_two).astype(LOW))
    gather_three = Gather(down_shards, gather_two.step())
    came = gather_three.step()
    hidden_two = jnp.concatenate(spread, axis=0)
    mlp_gate_full, mlp_up_full = gather_two.full()
    pre_mlp = project(hidden_two, mlp_gate_full)
    mlp_up_full = after_that(mlp_up_full, (came, pre_mlp))
    came = gather_three.step()
    pre_up = project(hidden_two, mlp_up_full)
    product = (gelu(pre_mlp) * pre_up).astype(LOW)
    grad_two = after_that(grad_two, (came, product))
    came = gather_three.step()
    down_part = outer_sum(grad_two, product)
    reduce_down = Reduce([down_part], gather_three.step())
    (mlp_down_full,) = gather_three.full()

    sent = reduce_down.step()
    grad_product = project(grad_two, after_that(mlp_down_full, sent))
    act, slope = gelu_parts(pre_mlp)
    grad_up = (grad_product * act).astype(LOW)
    grad_mlp = meet((grad_product * pre_up * slope).astype(LOW), reduce_down)
    sent = reduce_down.step()

    kept, away = back_project([after_that(grad_mlp, sent), grad_up], [mlp_gate_full, mlp_up_full])
    away = meet(away, reduce_down)
    sent = reduce_down.step()
    came = to_near(away)
    mlp_gate_part = outer_sum(after_that(hidden_two, (sent, away)), grad_mlp)
    kept, beyond = joined(kept, after_that(came, mlp_gate_part))
    beyond = meet(beyond, reduce_down)
    sent = reduce_down.step()
    arrived = to_far(beyond)
    mlp_up_part = outer_sum(after_that(hidden_two, (sent, beyond)), grad_up)
    result_kept, result_away = back_project([after_that(product, mlp_up_part)], [mlp_down_full])
    arrived = meet(after_that(arrived, result_away), reduce_down)
    reduce_gate = Reduce([mlp_gate_part], reduce_down.latest)
    reduce_up = Reduce([mlp_up_part], reduce_down.latest)
    sent = (reduce_gate.step(), reduce_up.step())
    back_two, share_two = norm_back(kept + arrived.astype(F32), after, root_two, gain_two)
    grad_after = cotangent_own + back_two
    own = after_that(grad_after.astype(LOW), sent)
    far, near = to_far(own), to_near(own)
    result_came = to_near(after_that(result_away, own))
    (grad_down,) = reduce_down.sums()
    grad_down = meet(grad_down, reduce_gate, reduce_up)
    sent = (reduce_gate.step(), reduce_up.step())
    far = after_that(far, sent)
    grad_one = jnp.concatenate([own, far, near, to_near(far)], axis=0)

    grad_mixed = project(after_that(grad_one, sent), output_full)
    grad_pre_gate, tail_decay, grad_part, export = run_backscan(
        grad_mixed, pre, state, recur, masks, coef
    )
    export = meet(export, reduce_gate, reduce_up)
    sent = (reduce_gate.step(), reduce_up.step())
    result_kept, result_beyond = joined(result_kept, after_that(result_came, (export, sent)))
    result_arrived = to_far(result_beyond)
    incoming = after_that(carried(export, True), result_beyond)[:, None, :]
    grad_pre, tail, head, gate_grads, sums = run_backward(
        tail_decay, grad_part, incoming, state, carry, recur, gate, conv, pre, halo, masks,
        conv_weight, coef, high, low, grad_pre_gate,
    )
    head = meet(after_that(head, result_arrived), reduce_gate, reduce_up)
    sent = reduce_gate.step()
    beyond = lax.ppermute(head, "seq", [(s + 1, s) for s in range(seq_count - 1)])
    result_delta = after + (result_kept + after_that(result_arrived, (sent, head)).astype(F32))
    result_delta = (result_delta - tokens_own).astype(LOW)
    result_far, result_near = to_far(result_delta), to_near(result_delta)
    out_part = outer_sum(grad_one, after_that(mixed, result_delta))
    beyond = after_that(beyond, out_part)
    grad_pre = lax.dynamic_update_slice(grad_pre, (tail + beyond).astype(LOW), (0, length - 8, 0))
    kept, away = back_project([grad_pre], [in_gate])
    away = meet(away, reduce_gate)
    reduce_up.others = away
    sent = reduce_up.step()
    came = to_near(away)
    gate_part = outer_sum(after_that(hidden_one, sent), grad_pre_gate)
    sum_rows = sums.astype(LOW).reshape(-1, WINDOW)
    small = jnp.concatenate(
        [
            gate_grads.reshape(-1, WINDOW),
            jnp.pad(sum_rows, ((0, -sum_rows.shape[0] % seq_count), (0, 0))),
        ]
    )
    small = after_that(small.reshape(seq_count, -1, WINDOW), away)
    small = lax.all_to_all(small, "seq", 0, 0, tiled=True)
    small = jnp.sum(small.astype(F32), axis=0)
    kept, beyond = joined(kept, after_that(came, gate_part))
    arrived = to_far(beyond)
    every = to_all(after_that(small, beyond).astype(LOW), "seq")
    result_pieces = [result_delta, result_far, result_near, to_near(after_that(result_far, beyond))]

    in_part = outer_sum(after_that(hidden_one, beyond), grad_pre[:, :, :channels])
    in_part = meet(in_part, reduce_up)
    reduce_branch = Reduce([out_part, gate_part, in_part], reduce_up.latest)
    sent = reduce_branch.step()

    arrived = after_that(arrived, sent)
    back_one, share_one = norm_back(
        kept + arrived.astype(F32), tokens_own, inverse_root(tokens_own), gain_one
    )
    token_own = meet(grad_after + back_one, reduce_branch)
    sent = reduce_branch.step()
    own = (token_own - cotangent_own).astype(LOW)
    far, near = to_far(own), to_near(own)
    shares = jnp.stack([features_back(share_one), features_back(share_two)]).reshape(-1, WINDOW)
    every_share = to_all(after_that(shares, own), ("seq", "ch"))
    (grad_mlp_gate_w,) = reduce_gate.sums()
    (grad_mlp_up_w,) = reduce_up.sums()
    far = meet(after_that(far, (grad_mlp_gate_w, grad_mlp_up_w)), reduce_branch)
    sent = reduce_branch.step()
    late_maps = after_that(maps, (sent, far))
    token_grad = assemble(cotangent, [own, far, near, to_near(far)], late_maps)
    late_maps = after_that(maps, token_grad)
    result = assemble(tokens, result_pieces, late_maps)
    result = meet(result, reduce_branch)
    reduce_branch.step()
    every, every_share = after_that((every, every_share), result)
    every = every.astype(F32)
    grad_out_w, grad_gate_w, grad_in_w = reduce_branch.sums()
    norm_shares = jnp.sum(every_share, axis=0).reshape(2, width)
    every = every.reshape(-1, WINDOW)
    size = channels // blocks
    gate_w = every[: 2 * channels].reshape(2 * blocks, size, WINDOW)[:, :, :size]
    sums = every[2 * channels : 2 * channels + sum_rows.shape[0]].reshape(sums.shape)
    swapped = turn // 2 + turn % 2 * 2
    block_states = jnp.concatenate(
        [
            lax.dynamic_slice_in_dim(state[:, -1:, :], swapped ^ row, 1, axis=0)
            for row in ROW_ORDER
        ],
        axis=0,
    )
    return (
        result,
        block_states,
        token_grad,
        norm_shares[0],
        grad_gate_w,
        grad_in_w,
        grad_out_w.T,
        sums[1:5],
        sums[0],
        8.0 * jax.nn.sigmoid(-decay_param) * sums[5],
        gate_w[:blocks],
        sums[6],
        gate_w[blocks:],
        sums[7],
        norm_shares[1],
        grad_mlp_gate_w,
        grad_mlp_up_w,
        grad_down.T,
    )


def solution(mesh):
    in_specs = (
        P(None, "seq", None),
        P(None, "seq", None),
        P(),
        P(),
        P("seq", "ch"),
        P("seq", "ch"),
        P("ch", "seq"),
        P(None, "ch"),
        P("ch"),
        P("ch"),
        P("ch", None, None),
        P("ch"),
        P("ch", None, None),
        P("ch"),
        P(),
        P("seq", "ch"),
        P("seq", "ch"),
        P("ch", "seq"),
    )
    out_specs = (
        P(None, "seq", None),
        P(None, "seq", "ch"),
        P(None, "seq", None),
        P(),
        P("seq", "ch"),
        P("seq", "ch"),
        P("ch", "seq"),
        P(None, "ch"),
        P("ch"),
        P("ch"),
        P("ch", None, None),
        P("ch"),
        P("ch", None, None),
        P("ch"),
        P(),
        P("seq", "ch"),
        P("seq", "ch"),
        P("ch", "seq"),
    )
    return jax.shard_map(body, mesh=mesh, in_specs=in_specs, out_specs=out_specs, check_vma=False)
```

```python
import jax
import jax.numpy as jnp
from jax import lax
from jax.experimental import pallas as pl
from jax.experimental.pallas import tpu as pltpu
from jax.sharding import PartitionSpec as P

LOW = jnp.bfloat16
F32 = jnp.float32
EPS = 1e-06
GELU_A = 0.7978845608028654
GELU_B = 0.044715
VMEM_LIMIT = 48 * 1024 * 1024
RING_LIMIT = 8
WINDOW = 256
SMALL_COST = pl.CostEstimate(flops=1, bytes_accessed=1, transcendentals=0)


def ring_order(count):
    return list(range(0, count, 2)) + list(range(count - 1, 0, -2))


def ring_place(seq_index, count):
    return jnp.where(seq_index % 2 == 0, seq_index // 2, count - 1 - seq_index // 2)


def ring_member(place, count):
    place = place % count
    return jnp.where(place < count // 2, 2 * place, 2 * (count - 1 - place) + 1)


def ring_pairs(count):
    order = ring_order(count)
    ahead = [(order[i], order[(i + 1) % count]) for i in range(count)]
    behind = [(target, source) for source, target in ahead]
    return ahead, behind


def ring_blocks(count):
    if count > RING_LIMIT:
        return [jnp.int32(0)]
    here = ring_place(lax.axis_index("seq"), count)
    offsets = [0]
    for step in range(1, count // 2):
        offsets += [-step, step]
    return [ring_member(here + offset, count) for offset in offsets + [count // 2]]


def ring_block(offset, count):
    if abs(offset) == count // 2:
        return count - 1
    return 2 * offset if offset >= 0 else -2 * offset - 1


def after_that(value, others):
    return lax.optimization_barrier((value, others))[0]


def meet(value, *rings):
    value, pieces = lax.optimization_barrier((value, [ring.latest for ring in rings]))
    for ring, came in zip(rings, pieces, strict=True):
        ring.replace(came)
    return value


class Gather:
    def __init__(self, shards, others=()):
        self.count = lax.axis_size("seq")
        self.shards = shards
        joined = jnp.concatenate(shards, axis=1) if len(shards) > 1 else shards[0]
        self.latest, self.others = (joined, joined), others
        self.up, self.down = [self.latest[0]], [self.latest[1]]

    def replace(self, pieces):
        self.latest = pieces
        if self.count <= RING_LIMIT:
            self.up[-1], self.down[-1] = pieces

    def step(self):
        if self.count <= RING_LIMIT and len(self.up) <= self.count // 2:
            ahead, behind = ring_pairs(self.count)
            cut = self.shards[0].shape[0] // 2
            first, second = self.latest
            if len(self.up) == self.count // 2:
                first, second = first[:cut], second[cut:]
            first, second = after_that((first, second), self.others)
            self.others = ()
            self.up.append(lax.ppermute(first, "seq", ahead))
            self.down.append(lax.ppermute(second, "seq", behind))
            self.latest = (self.up[-1], self.down[-1])
        return self.latest

    def full(self):
        if self.count > RING_LIMIT:
            return [lax.all_gather(shard, "seq", axis=0, tiled=True) for shard in self.shards]
        pieces = [self.up[0]]
        for first, second in zip(self.up[1:], self.down[1:], strict=True):
            pieces += [first, second]
        full, start = [], 0
        for shard in self.shards:
            stop = start + shard.shape[1]
            full.append(jnp.concatenate([piece[:, start:stop] for piece in pieces], axis=0))
            start = stop
        return full


class Reduce:
    def __init__(self, fulls, others=()):
        self.count = lax.axis_size("seq")
        self.fulls = fulls
        self.left = self.count // 2
        self.latest, self.sent = (), ()
        self.others = others

    def replace(self, pieces):
        self.latest = pieces

    def step(self):
        if self.count <= RING_LIMIT and self.left > 0:
            ahead, behind = ring_pairs(self.count)
            up, down = ring_step(self.fulls, self.latest, self.count, self.left)
            up, down = after_that((up, down), self.others)
            self.others = ()
            self.sent = (up, down)
            self.latest = (lax.ppermute(up, "seq", ahead), lax.ppermute(down, "seq", behind))
            self.left -= 1
        return self.sent

    def sums(self):
        if self.count > RING_LIMIT:
            return [
                lax.psum_scatter(full.astype(F32), "seq", scatter_dimension=0, tiled=True)
                for full in self.fulls
            ]
        return ring_step(self.fulls, self.latest, self.count, 0)


def ring_step(fulls, came, count, step):
    half, rows = count // 2, fulls[0].shape[0] // count
    widths = [full.shape[1] for full in fulls]
    total = sum(widths)
    parts = 2
    piece = rows // parts
    first, last = step == half, step == 0

    def kernel(*refs):
        ups, downs = refs[: len(fulls)], refs[len(fulls) : 2 * len(fulls)]
        rest = refs[2 * len(fulls) :]
        got, out = rest[: len(came)], rest[len(came) :]
        place = pl.program_id(0)
        start = 0
        for index, width in enumerate(widths):
            columns = slice(start, start + width)
            start += width
            up, down = ups[index][...].astype(F32), downs[index][...].astype(F32)
            if last:
                out[index][...] = up + got[0][:, columns].astype(F32) + got[1][:, columns].astype(F32)
                continue
            if not first:
                plus, minus = got[0][:, columns].astype(F32), got[1][:, columns].astype(F32)
                if step == half - 1:
                    plus = jnp.where(place < parts // 2, plus, 0.0)
                    minus = jnp.where(place >= parts // 2, minus, 0.0)
                up, down = up + plus, down + minus
            out[0][:, columns] = up.astype(LOW)
            out[1][:, columns] = down.astype(LOW)

    def at(place, offset=0):
        block = ring_block(place, count)
        return lambda i: (block * parts + i + offset, 0)

    grid = parts // 2 if first else parts
    blocks = [pl.BlockSpec((piece, w), at(step)) for w in widths]
    blocks += [pl.BlockSpec((piece, w), at(-step, parts // 2 if first else 0)) for w in widths]
    got_specs = [pl.BlockSpec((piece, total), lambda i: (i, 0))] * len(came)
    if step == half - 1:
        got_specs = [
            pl.BlockSpec((piece, total), lambda i: (jnp.minimum(i, parts // 2 - 1), 0)),
            pl.BlockSpec((piece, total), lambda i: (jnp.maximum(i - parts // 2, 0), 0)),
        ]
    if last:
        out_specs = [pl.BlockSpec((piece, w), lambda i: (i, 0)) for w in widths]
        out_shape = [shape_of((rows, w)) for w in widths]
    else:
        out_specs = [pl.BlockSpec((piece, total), lambda i: (i, 0))] * 2
        out_shape = [shape_of((grid * piece, total), LOW)] * 2
    return pl.pallas_call(
        kernel, grid=(grid,), in_specs=blocks + got_specs, out_specs=out_specs,
        out_shape=out_shape, compiler_params=params(), cost_estimate=SMALL_COST, name="ring_step",
    )(*fulls, *fulls, *came)


ROW_ORDER = (0, 2, 1, 3)


def near_pairs(count):
    return [(c, c ^ 1) for c in range(count)]


def far_pairs(count):
    return [(c, c ^ 2) for c in range(count)]


def to_near(value):
    return lax.ppermute(value, "ch", near_pairs(lax.axis_size("ch")))


def to_far(value):
    return lax.ppermute(value, "ch", far_pairs(lax.axis_size("ch")))


def spread_rows(own):
    far, near = to_far(own), to_near(own)
    return [own, far, near, to_near(far)]


def sum_over(value, axis, dtype=F32):
    count, step = lax.axis_size(axis), 1
    while step < count:
        sent = value.astype(dtype)
        came = lax.ppermute(sent, axis, [(c, c ^ step) for c in range(count)])
        value = sent.astype(F32) + came.astype(F32)
        step *= 2
    return value


def carried(ends, backward):
    count, mine = lax.axis_size("seq"), lax.axis_index("seq")
    pieces = to_all(ends[:, :2].reshape(-1, ends.shape[2]), "seq").reshape(
        count, ends.shape[0], 2, ends.shape[2]
    )
    total = jnp.zeros_like(ends[:, 0])
    for place in range(count - 1):
        member = count - 1 - place if backward else place
        counts = member > mine if backward else member < mine
        piece = pieces[member]
        total = jnp.where(counts, piece[:, 0] * total + piece[:, 1], total)
    return total


def to_all(value, axis):
    count = lax.axis_size(axis)
    return lax.all_to_all(
        jnp.broadcast_to(value[None], (count,) + value.shape), axis, 0, 0, tiled=True
    )


def row_block(shape, column=0):
    return pl.BlockSpec((1,) + shape, lambda row, *_: (row, 0, column))


def whole_block(shape):
    return pl.BlockSpec(shape, lambda row, *_: (0,) * len(shape))


def gelu_parts(value):
    tanh = jnp.tanh(GELU_A * (value + GELU_B * value * value * value))
    act = 0.5 * value * (1.0 + tanh)
    slope = 0.5 * (1.0 + tanh) + 0.5 * value * (1.0 - tanh * tanh) * GELU_A * (
        1.0 + 3.0 * GELU_B * value * value
    )
    return act, slope


def gelu(value):
    return gelu_parts(value)[0]


def minus_expm1(value):
    series = jnp.full_like(value, 1.0 / 11.0)
    for divisor in range(10, 1, -1):
        series = (1.0 + value * series) * (1.0 / divisor)
    series = -value * (1.0 + value * series)
    return jnp.where(value > -0.8, series, 1.0 - jnp.exp(value))


def split(value):
    high = value.astype(LOW)
    return high, (value - high.astype(F32)).astype(LOW)


def dot(left, right, contract):
    return lax.dot_general(left, right, (contract, ((), ())), preferred_element_type=F32)


def dot_three(left, right, contract):
    (left_high, left_low), (right_high, right_low) = left, right
    return (
        dot(left_high, right_high, contract)
        + dot(left_high, right_low, contract)
        + dot(left_low, right_high, contract)
    )


def windows(count, size):
    starts = [min(block * size // 128 * 128, count * size - WINDOW) for block in range(count)]
    return [(start, block * size - start) for block, start in enumerate(starts)]


def window_dots(value, high_ref, low_ref, first, spots, contract):
    parts = []
    for index, (start, _) in enumerate(spots):
        piece = split(value[:, start : start + WINDOW])
        weight = (high_ref[first + index], low_ref[first + index])
        parts.append((start, dot_three(piece, weight, contract)))
    columns = []
    for tile in range(0, value.shape[1], 128):
        total = None
        for start, part in parts:
            if start <= tile < start + WINDOW:
                share = part[:, tile - start : tile - start + 128]
                total = share if total is None else total + share
        columns.append(total)
    return jnp.concatenate(columns, axis=1)


def decay_and_factor(recur, coef, reset):
    log_decay = coef * recur
    plain = jnp.exp(log_decay)
    decay = jnp.where(reset, 0.0, plain)
    factor = jnp.where(reset, 1.0, jnp.sqrt(minus_expm1(2.0 * log_decay)))
    return plain, decay, factor


def tile_scan(alpha, beta, backward):
    place = lax.broadcasted_iota(jnp.int32, alpha.shape, 1)
    for step in (1, 2, 4):
        turn = 8 - step if backward else step
        inside = place < 8 - step if backward else place >= step
        other_alpha = pltpu.roll(alpha, turn, 1)
        other_beta = pltpu.roll(beta, turn, 1)
        beta = jnp.where(inside, alpha * other_beta + beta, beta)
        alpha = jnp.where(inside, alpha * other_alpha, alpha)
    return alpha, beta


def join_tiles(alpha_ref, beta_ref, backward):
    length, channels = alpha_ref.shape[1], alpha_ref.shape[2]
    groups = length // 8

    def step(index, carry):
        alpha_carry, beta_carry = carry
        group = groups - 1 - index if backward else index
        rows = pl.ds(pl.multiple_of(group * 8, 8), 8)
        alpha, beta = alpha_ref[0, rows, :], beta_ref[0, rows, :]
        beta = alpha * beta_carry + beta
        alpha = alpha * alpha_carry
        alpha_ref[0, rows, :] = alpha
        beta_ref[0, rows, :] = beta
        last = 0 if backward else 7
        return alpha[last : last + 1], beta[last : last + 1]

    start = (jnp.ones((1, channels), F32), jnp.zeros((1, channels), F32))
    return lax.fori_loop(0, groups, step, start, unroll=4)


def forward_kernel(
    input_ref, halo_ref, mask_ref, taps_ref, bias_ref, coef_ref, high_ref, low_ref, gate_bias_ref,
    conv_ref, recur_ref, gate_ref, alpha_ref, beta_ref, export_ref, extended,
):
    length, channels = input_ref.shape[1], input_ref.shape[2]
    extended[0:8, :] = halo_ref[0]
    extended[8 : 8 + length, :] = input_ref[0]
    masks = mask_ref[0]
    conv = bias_ref[...] + taps_ref[0:1, :] * input_ref[0]
    for lag in (1, 2, 3):
        lagged = extended[8 - lag : 8 - lag + length, :]
        conv = conv + taps_ref[lag : lag + 1, :] * lagged * masks[:, lag : lag + 1]
    conv_ref[0] = conv
    count = high_ref.shape[0] // 2
    spots = windows(count, channels // count)
    before = [
        window_dots(conv, high_ref, low_ref, first, spots, ((1,), (0,))) for first in (0, count)
    ]
    recur = jax.nn.sigmoid(before[0] + gate_bias_ref[:, :channels])
    gate = jax.nn.sigmoid(before[1] + gate_bias_ref[:, channels:])
    recur_ref[0] = recur
    gate_ref[0] = gate
    reset = masks[:, 0:1] > 0.5
    _, decay, factor = decay_and_factor(recur, coef_ref[...], reset)
    driven = factor * gate * conv
    grouped = (length // 8, 8, channels)
    alpha, beta = tile_scan(decay.reshape(grouped), driven.reshape(grouped), False)
    alpha_ref[0] = alpha.reshape(length, channels)
    beta_ref[0] = beta.reshape(length, channels)
    alpha, beta = join_tiles(alpha_ref, beta_ref, False)
    export_ref[0] = jnp.concatenate([alpha, beta, jnp.zeros((6, channels), F32)], axis=0)


def backscan_kernel(
    mixed_ref, pre_ref, state_ref, recur_ref, mask_ref, coef_ref,
    pre_grad_ref, alpha_ref, beta_ref, export_ref, extended,
):
    length, channels = mixed_ref.shape[1], mixed_ref.shape[2]
    act, slope = gelu_parts(pre_ref[0])
    mixed = mixed_ref[0]
    pre_grad_ref[0] = (mixed * state_ref[0] * slope).astype(LOW)
    reset = mask_ref[0][:, 0:1] > 0.5
    decay = jnp.where(reset, 0.0, jnp.exp(coef_ref[...] * recur_ref[0]))
    extended[0:length, :] = decay
    extended[length : length + 8, :] = jnp.ones((8, channels), F32)
    following = extended[1 : 1 + length, :]
    grouped = (length // 8, 8, channels)
    alpha, beta = tile_scan(following.reshape(grouped), (mixed * act).reshape(grouped), True)
    alpha_ref[0] = alpha.reshape(length, channels)
    beta_ref[0] = beta.reshape(length, channels)
    alpha, beta = join_tiles(alpha_ref, beta_ref, True)
    first = extended[0:1, :]
    export_ref[0] = jnp.concatenate(
        [first * alpha, first * beta, jnp.zeros((6, channels), F32)], axis=0
    )


def backward_kernel(
    alpha_ref, beta_ref, incoming_ref, state_ref, carry_ref, recur_ref, gate_ref, conv_ref,
    input_ref, halo_ref, mask_ref, taps_ref, coef_ref, high_ref, low_ref, pre_grad_ref,
    grad_ref, tail_ref, head_ref, weight_ref, sums_ref, extended, masked, weight_acc,
):
    length, channels = alpha_ref.shape[1], alpha_ref.shape[2]

    @pl.when(pl.program_id(0) == 0)
    def _():
        weight_acc[...] = jnp.zeros_like(weight_acc)
        sums_ref[...] = jnp.zeros_like(sums_ref)

    masks = mask_ref[0]
    reset = masks[:, 0:1] > 0.5
    recur, gate, conv, coef = recur_ref[0], gate_ref[0], conv_ref[0], coef_ref[...]
    plain, decay, factor = decay_and_factor(recur, coef, reset)
    grad = beta_ref[0] + alpha_ref[0] * incoming_ref[0]
    extended[0:8, :] = jnp.broadcast_to(carry_ref[0], (8, channels))
    extended[8 : 8 + length, :] = state_ref[0]
    prior = extended[7 : 7 + length, :]
    grad_decay = grad * prior
    grad_factor = grad * gate * conv
    grad_log = jnp.where(reset, 0.0, grad_decay * decay - grad_factor * plain * plain / factor)
    grad_recur = coef * grad_log * recur * (1.0 - recur)
    grad_gate = grad * factor * conv * gate * (1.0 - gate)
    count = high_ref.shape[0] // 2
    size = channels // count
    spots = windows(count, size)
    grad_conv = grad * factor * gate
    for first, values in ((0, grad_recur), (count, grad_gate)):
        for index, (start, _) in enumerate(spots):
            columns = slice(start, start + WINDOW)
            pair = split(conv[:, columns]), split(values[:, columns])
            weight_acc[first + index] += dot_three(*pair, ((0,), (0,)))
        grad_conv = grad_conv + window_dots(
            values, high_ref, low_ref, first, spots, ((1,), (1,))
        )

    @pl.when(pl.program_id(0) == pl.num_programs(0) - 1)
    def _():
        for index in range(2 * count):
            place = spots[index % count][1]
            turned = weight_acc[index]
            if place:
                turned = pltpu.roll(turned, WINDOW - place, 1)
            weight_ref[index] = turned[place : place + size].astype(LOW)


    def total(value):
        return jnp.sum(value, axis=0, keepdims=True)

    extended[0:8, :] = halo_ref[0]
    extended[8 : 8 + length, :] = input_ref[0]
    sums = [total(grad_conv), total(grad_conv * input_ref[0])]
    masked[0:8, :] = jnp.zeros((8, channels), F32)
    masked[8 + length : 16 + length, :] = jnp.zeros((8, channels), F32)
    spread = taps_ref[0:1, :] * grad_conv
    head = jnp.zeros((8, channels), F32)
    for lag in (1, 2, 3):
        kept = grad_conv * masks[:, lag : lag + 1]
        sums.append(total(kept * extended[8 - lag : 8 - lag + length, :]))
        masked[8 : 8 + length, :] = kept
        tap = taps_ref[lag : lag + 1, :]
        spread = spread + tap * masked[8 + lag : 8 + lag + length, :]
        head = head + tap * masked[lag : 8 + lag, :]
    sums += [total(recur * grad_log), total(grad_recur), total(grad_gate)]
    sums_ref[...] += jnp.concatenate(sums, axis=0)
    grad_ref[0, :, :channels] = spread.astype(LOW)
    grad_ref[0, :, channels:] = pre_grad_ref[0]
    tail_ref[0] = spread[length - 8 :, :]
    head_ref[0] = head


def params():
    return pltpu.CompilerParams(
        dimension_semantics=("arbitrary",), vmem_limit_bytes=VMEM_LIMIT
    )


def shape_of(shape, dtype=F32):
    return jax.ShapeDtypeStruct(shape, dtype)


def run_forward(pre, halo, masks, taps, bias, coef, high, low, gate_bias):
    rows, length, channels = pre.shape[0], pre.shape[1], taps.shape[1]
    block = row_block((length, channels))
    return pl.pallas_call(
        forward_kernel,
        grid=(rows,),
        in_specs=[
            block, row_block((8, channels)), row_block((length, 8)), whole_block((4, channels)),
            whole_block((1, channels)), whole_block((1, channels)), whole_block(high.shape),
            whole_block(low.shape), whole_block((1, 2 * channels)),
        ],
        out_specs=[block] * 5 + [row_block((8, channels))],
        out_shape=[shape_of((rows, length, channels))] * 5 + [shape_of((rows, 8, channels))],
        scratch_shapes=[pltpu.VMEM((length + 8, channels), F32)],
        compiler_params=params(), cost_estimate=SMALL_COST,
        name="forward_scan",
    )(pre, halo, masks, taps, bias, coef, high, low, gate_bias)


def run_backscan(mixed, pre, state, recur, masks, coef):
    rows, length, channels = mixed.shape
    block = row_block((length, channels))
    return pl.pallas_call(
        backscan_kernel,
        grid=(rows,),
        in_specs=[
            block, row_block((length, channels), 1), block, block, row_block((length, 8)),
            whole_block((1, channels)),
        ],
        out_specs=[block] * 3 + [row_block((8, channels))],
        out_shape=[
            shape_of(mixed.shape, LOW), shape_of(mixed.shape), shape_of(mixed.shape),
            shape_of((rows, 8, channels)),
        ],
        scratch_shapes=[pltpu.VMEM((length + 8, channels), F32)],
        compiler_params=params(), cost_estimate=SMALL_COST,
        name="backward_scan",
    )(mixed, pre, state, recur, masks, coef)


def run_backward(
    alpha, beta, incoming, state, carry, recur, gate, conv, pre, halo, masks, taps, coef, high, low, pre_grad
):
    rows, length, channels = alpha.shape
    block, edge, line = (
        row_block((length, channels)), row_block((8, channels)), row_block((1, channels)),
    )
    weights = (high.shape[0], 2 * channels // high.shape[0], WINDOW)
    return pl.pallas_call(
        backward_kernel,
        grid=(rows,),
        in_specs=[
            block, block, line, block, line, block, block, block, block, edge,
            row_block((length, 8)), whole_block((4, channels)), whole_block((1, channels)),
            whole_block(high.shape), whole_block(low.shape), block,
        ],
        out_specs=[row_block((length, 2 * channels)), edge, edge, whole_block(weights), whole_block((8, channels))],
        out_shape=[
            shape_of((rows, length, 2 * channels), LOW), shape_of((rows, 8, channels)),
            shape_of((rows, 8, channels)), shape_of(weights, LOW), shape_of((8, channels)),
        ],
        scratch_shapes=[
            pltpu.VMEM((length + 8, channels), F32), pltpu.VMEM((length + 16, channels), F32),
            pltpu.VMEM(high.shape, F32),
        ],
        compiler_params=params(), cost_estimate=SMALL_COST,
        name="branch_backward",
    )(alpha, beta, incoming, state, carry, recur, gate, conv, pre, halo, masks, taps, coef, high, low, pre_grad)


def back_project(lefts, rights):
    rows, length, _ = lefts[0].shape
    width, tile = rights[0].shape[0], 256
    half = rows // 2

    def kernel(*refs):
        total = None
        for left, right in zip(refs[: len(lefts)], refs[len(lefts) : 2 * len(lefts)], strict=True):
            flat = left[...].reshape(rows * length, left.shape[2])
            share = dot(flat, right[...], ((1,), (1,)))
            total = share if total is None else total + share
        total = total.reshape(rows, length, tile)
        refs[-2][...] = total[:half]
        refs[-1][...] = total[half:].astype(LOW)

    out = pl.BlockSpec((half, length, tile), lambda i: (0, 0, i))
    in_specs = [pl.BlockSpec(left.shape, lambda i: (0, 0, 0)) for left in lefts]
    in_specs += [pl.BlockSpec((tile, right.shape[1]), lambda i: (i, 0)) for right in rights]
    return pl.pallas_call(
        kernel, grid=(width // tile,), in_specs=in_specs, out_specs=[out, out],
        out_shape=[shape_of((half, length, width)), shape_of((half, length, width), LOW)],
        compiler_params=params(), cost_estimate=SMALL_COST, name="back_project",
    )(*lefts, *rights)


def joined(kept, came):
    total = kept + came.astype(F32)
    return total[0:1], total[1:2].astype(LOW)


def part(index, width):
    return pl.ds(pl.multiple_of(index * width, 128), width)


def norm_kernel(row_map, block_map, gain_ref, values_ref, out_ref):
    blocks = block_map.shape[0]
    width = values_ref.shape[2] // blocks
    values = values_ref[0]
    root = lax.rsqrt(jnp.mean(values * values, axis=-1, keepdims=True) + EPS)
    for place in range(blocks):
        there = part(block_map[place], width)
        normed = values_ref[0, :, there] * root * gain_ref[:, there]
        out_ref[0, :, place * width : (place + 1) * width] = normed.astype(LOW)


def relative_kernel(row_map, block_map, values_ref, own_ref, *out_refs):
    blocks = block_map.shape[0]
    width = values_ref.shape[2] // blocks
    for place in range(blocks):
        there = part(block_map[place], width)
        here = slice(place * width, (place + 1) * width)
        for out_ref in out_refs:
            out_ref[0, :, here] = values_ref[0, :, there].astype(LOW)

        @pl.when(pl.program_id(0) == 0)
        def _():
            own_ref[0, :, here] = values_ref[0, :, there]


def assemble_kernel(row_map, block_map, base_ref, *refs):
    pieces, out_ref = refs[:-1], refs[-1]
    blocks = block_map.shape[0]
    width = base_ref.shape[2] // blocks
    for row, piece in enumerate(pieces):

        @pl.when(pl.program_id(0) == row)
        def _():
            for place in range(blocks):
                there = part(block_map[place], width)
                here = slice(place * width, (place + 1) * width)
                out_ref[0, :, there] = base_ref[0, :, there] + piece[0, :, here].astype(F32)


def arranged(kernel, maps, out_shape, in_specs, out_specs, *arrays):
    return pl.pallas_call(
        kernel,
        grid_spec=pltpu.PrefetchScalarGridSpec(
            num_scalar_prefetch=2, grid=(maps[0].shape[0],), in_specs=in_specs, out_specs=out_specs
        ),
        out_shape=out_shape,
        compiler_params=params(), cost_estimate=SMALL_COST,
    )(*maps, *arrays)


def mapped_row(shape):
    return pl.BlockSpec((1,) + shape, lambda row, row_map, block_map: (row_map[row], 0, 0))


def relative_norm(values, gain, maps):
    shape = values.shape[1:]
    return arranged(
        norm_kernel, maps, shape_of(values.shape, LOW),
        [whole_block((1, shape[1])), mapped_row(shape)], row_block(shape), gain[None, :], values,
    )


def relative_rows(values, maps, rounded):
    shape = values.shape[1:]
    shapes, specs = [shape_of((1,) + shape)], [whole_block((1,) + shape)]
    if rounded:
        shapes, specs = shapes + [shape_of(values.shape, LOW)], specs + [row_block(shape)]
    if not rounded:
        maps = (maps[0][:1], maps[1])
    return arranged(relative_kernel, maps, shapes, [mapped_row(shape)], specs, values)


def assemble(base, pieces, maps):
    shape = base.shape[1:]
    return arranged(
        assemble_kernel, maps, shape_of(base.shape),
        [mapped_row(shape)] + [whole_block((1,) + shape)] * len(pieces), mapped_row(shape),
        base, *pieces,
    )


def project(left, right):
    return jnp.einsum("rtd,df->rtf", left, right, preferred_element_type=F32)


def project_back(left, right):
    return jnp.einsum("rtf,df->rtd", left, right, preferred_element_type=F32)


def outer_sum(left, right):
    return jnp.einsum("rtd,rtf->df", left, right, preferred_element_type=F32).astype(LOW)


def inverse_root(values):
    return lax.rsqrt(jnp.mean(values * values, axis=-1, keepdims=True) + EPS)


def norm_back(grad, values, root, gain):
    scaled = grad * gain
    inner = jnp.mean(scaled * values, axis=-1, keepdims=True)
    share = jnp.sum(grad * values * root, axis=(0, 1))
    return root * scaled - values * (root * root * root) * inner, share


def gate_matrix_kernel(recur_ref, input_ref, high_ref, low_ref):
    count, size = recur_ref.shape[0], recur_ref.shape[1]
    high_ref[...] = jnp.zeros_like(high_ref)
    low_ref[...] = jnp.zeros_like(low_ref)
    for index, ref in enumerate((recur_ref, input_ref)):
        for block, (_, place) in enumerate(windows(count, size)):
            high, low = split(ref[block])
            here = slice(place, place + size)
            high_ref[index * count + block, here, here] = high
            low_ref[index * count + block, here, here] = low


def gate_matrix(recur_weight, input_weight):
    shape = shape_of((2 * recur_weight.shape[0], WINDOW, WINDOW), LOW)
    return pl.pallas_call(
        gate_matrix_kernel, out_shape=[shape, shape],
        compiler_params=pltpu.CompilerParams(vmem_limit_bytes=VMEM_LIMIT), cost_estimate=SMALL_COST, name="gate_matrix",
    )(recur_weight, input_weight)


def body(
    tokens, cotangent, doc_starts, norm1_gain, branch_gate_w, branch_in_w, branch_out_w,
    conv_weight, conv_bias, decay_param, recur_gate_w, recur_gate_b, input_gate_w, input_gate_b,
    norm2_gain, mlp_gate_w, mlp_up_w, mlp_down_w,
):
    rows, length, width = tokens.shape
    channels, blocks = conv_bias.shape[0], recur_gate_w.shape[0]
    seq_count = lax.axis_size("seq")
    mine, turn = lax.axis_index("seq"), lax.axis_index("ch")
    row_map = jnp.stack([turn ^ row for row in ROW_ORDER]).astype(jnp.int32)
    block_map = jnp.stack(ring_blocks(seq_count)).astype(jnp.int32)
    maps = (row_map, block_map)

    def row_of(values, row):
        return lax.dynamic_slice_in_dim(values, turn ^ ROW_ORDER[row], 1, axis=0)

    def features(values):
        return jnp.take(values.reshape(block_map.shape[0], -1), block_map, axis=0).reshape(-1)

    def features_back(values):
        there = jnp.argmax(block_map[None, :] == jnp.arange(block_map.shape[0])[:, None], axis=1)
        return jnp.take(values.reshape(block_map.shape[0], -1), there, axis=0).reshape(-1)

    gather_one = Gather(
        [
            jnp.concatenate([branch_in_w.astype(LOW), branch_gate_w.astype(LOW)], axis=1),
            branch_out_w.astype(LOW).T,
        ]
    )
    came = gather_one.step()

    starts = jnp.concatenate([row_of(doc_starts, j) for j in range(rows)], axis=0)
    positions = mine * length - 3 + jnp.arange(length + 3, dtype=jnp.int32)
    reset_ext = jnp.any(starts[:, :, None] == positions[None, None, :], axis=1)
    blocked = reset_ext[:, 3:]
    columns = [blocked.astype(F32)]
    for lag in (1, 2, 3):
        columns.append(jnp.where(blocked, 0.0, 1.0))
        blocked = blocked | reset_ext[:, 3 - lag : 3 - lag + length]
    masks = jnp.stack(columns + [jnp.zeros_like(columns[0])] * 4, axis=-1)

    gate_bias = jnp.concatenate([recur_gate_b, input_gate_b])[None, :]
    coef = (-8.0 * jax.nn.softplus(-decay_param))[None, :]
    gain_one, gain_two = features(norm1_gain), features(norm2_gain)
    mlp_shards = [mlp_gate_w.astype(LOW), mlp_up_w.astype(LOW)]
    down_shards = [mlp_down_w.astype(LOW).T]

    before = after_that(tokens[:, -8:, :], came)
    before = lax.ppermute(before, "seq", [(s, s + 1) for s in range(seq_count - 1)])
    first_maps = after_that(maps, (came, masks))
    came = gather_one.step()
    hidden_one = relative_norm(tokens, norm1_gain, first_maps)
    hidden_before = relative_norm(before, norm1_gain, first_maps)
    recur_weights = after_that(recur_gate_w, (came, hidden_before))
    came = gather_one.step()
    high, low = gate_matrix(recur_weights, input_gate_w)
    gather_two = Gather(mlp_shards, gather_one.step())
    gather_two.step()
    in_gate, output_full = gather_one.full()

    pre = project(hidden_one, in_gate)
    halo = project(hidden_before, in_gate)
    conv, recur, gate, decay_sum, state_part, export = run_forward(
        pre, halo, masks, conv_weight, conv_bias[None, :], coef, high, low, gate_bias
    )
    export = meet(export, gather_two)
    carry = carried(export, False)[:, None, :]
    came = gather_two.step()
    state = state_part + decay_sum * carry
    mixed = (gelu(pre[:, :, channels:]) * state).astype(LOW)

    kept, away = back_project([mixed], [output_full])
    kept, beyond = joined(kept, to_near(away))
    arrived = to_far(beyond)
    late_maps = after_that(maps, beyond)
    (tokens_own,) = relative_rows(tokens, late_maps, False)
    cotangent_own, grad_two = relative_rows(cotangent, late_maps, True)
    kept = meet(after_that(kept, (tokens_own, cotangent_own)), gather_two)
    after = tokens_own + (kept + arrived.astype(F32))
    came = gather_two.step()
    root_two = inverse_root(after)
    spread = spread_rows((after * root_two * gain_two).astype(LOW))
    gather_three = Gather(down_shards, gather_two.step())
    came = gather_three.step()
    hidden_two = jnp.concatenate(spread, axis=0)
    mlp_gate_full, mlp_up_full = gather_two.full()
    pre_mlp = project(hidden_two, mlp_gate_full)
    mlp_up_full = after_that(mlp_up_full, (came, pre_mlp))
    came = gather_three.step()
    pre_up = project(hidden_two, mlp_up_full)
    product = (gelu(pre_mlp) * pre_up).astype(LOW)
    grad_two = after_that(grad_two, (came, product))
    came = gather_three.step()
    down_part = outer_sum(grad_two, product)
    reduce_down = Reduce([down_part], gather_three.step())
    (mlp_down_full,) = gather_three.full()

    sent = reduce_down.step()
    grad_product = project(grad_two, after_that(mlp_down_full, sent))
    act, slope = gelu_parts(pre_mlp)
    grad_up = (grad_product * act).astype(LOW)
    grad_mlp = meet((grad_product * pre_up * slope).astype(LOW), reduce_down)
    sent = reduce_down.step()

    kept, away = back_project([after_that(grad_mlp, sent), grad_up], [mlp_gate_full, mlp_up_full])
    away = meet(away, reduce_down)
    sent = reduce_down.step()
    kept, beyond = joined(kept, after_that(to_near(away), sent))
    arrived = to_far(beyond)
    mlp_gate_part = outer_sum(after_that(hidden_two, beyond), grad_mlp)
    mlp_gate_part = meet(mlp_gate_part, reduce_down)
    sent = reduce_down.step()
    arrived = after_that(arrived, sent)
    back_two, share_two = norm_back(kept + arrived.astype(F32), after, root_two, gain_two)
    grad_after = cotangent_own + back_two
    own = grad_after.astype(LOW)
    far, near = to_far(own), to_near(own)
    mlp_up_part = outer_sum(after_that(hidden_two, own), grad_up)
    mlp_up_part = meet(mlp_up_part, reduce_down)
    reduce_gate = Reduce([mlp_gate_part], reduce_down.latest)
    sent = reduce_gate.step()
    result_kept, result_away = back_project(
        [after_that(product, (sent, mlp_up_part))], [mlp_down_full]
    )
    (grad_down,) = reduce_down.sums()
    result_away = meet(result_away, reduce_gate)
    reduce_up = Reduce([mlp_up_part], reduce_gate.latest)
    sent = (reduce_up.step(), reduce_gate.step())
    far = after_that(far, sent)
    result_came = to_near(after_that(result_away, far))
    grad_one = jnp.concatenate([own, far, near, to_near(far)], axis=0)

    grad_mixed = project(after_that(grad_one, sent), output_full)
    grad_pre_gate, tail_decay, grad_part, export = run_backscan(
        grad_mixed, pre, state, recur, masks, coef
    )
    export = meet(export, reduce_gate, reduce_up)
    incoming = carried(export, True)[:, None, :]
    result_kept, result_beyond = joined(result_kept, after_that(result_came, export))
    incoming = after_that(incoming, result_beyond)
    reduce_gate.others = reduce_up.others = incoming
    sent = (reduce_up.step(), reduce_gate.step())
    result_arrived = to_far(after_that(result_beyond, incoming))
    grad_pre, tail, head, gate_grads, sums = run_backward(
        tail_decay, grad_part, incoming, state, carry, recur, gate, conv, pre, halo, masks,
        conv_weight, coef, high, low, grad_pre_gate,
    )
    head = meet(after_that(head, result_arrived), reduce_up)
    sent = reduce_up.step()
    beyond = lax.ppermute(head, "seq", [(s + 1, s) for s in range(seq_count - 1)])
    result_delta = after + (result_kept + after_that(result_arrived, (sent, head)).astype(F32))
    result_delta = (result_delta - tokens_own).astype(LOW)
    result_far, result_near = to_far(result_delta), to_near(result_delta)
    out_part = outer_sum(grad_one, after_that(mixed, result_delta))
    beyond = after_that(beyond, out_part)
    grad_pre = lax.dynamic_update_slice(grad_pre, (tail + beyond).astype(LOW), (0, length - 8, 0))
    kept, away = back_project([grad_pre], [in_gate])
    away = meet(away, reduce_gate, reduce_up)
    reduce_gate.others = away
    sent = reduce_gate.step()
    came = to_near(away)
    gate_part = outer_sum(after_that(hidden_one, sent), grad_pre_gate)
    kept, beyond = joined(kept, after_that(came, gate_part))
    beyond = meet(beyond, reduce_gate)
    arrived = to_far(beyond)
    reduce_up.others = beyond
    sent = reduce_up.step()

    in_part = outer_sum(after_that(hidden_one, (sent, beyond)), grad_pre[:, :, :channels])
    sum_rows = sums.astype(LOW).reshape(-1, WINDOW)
    small = jnp.concatenate(
        [
            gate_grads.reshape(-1, WINDOW),
            jnp.pad(sum_rows, ((0, -sum_rows.shape[0] % seq_count), (0, 0))),
        ]
    )
    small = after_that(small.reshape(seq_count, -1, WINDOW), in_part)
    in_part = after_that(in_part, small)
    small = lax.all_to_all(small, "seq", 0, 0, tiled=True)
    small = jnp.sum(small.astype(F32), axis=0).astype(LOW)
    every = to_all(small, "seq")
    in_part = meet(in_part, reduce_gate, reduce_up)
    reduce_branch = Reduce([out_part, gate_part, in_part], reduce_up.latest)
    sent = reduce_branch.step()

    arrived = after_that(arrived, sent)
    back_one, share_one = norm_back(
        kept + arrived.astype(F32), tokens_own, inverse_root(tokens_own), gain_one
    )
    token_own = meet(grad_after + back_one, reduce_branch)
    sent = reduce_branch.step()
    own = (token_own - cotangent_own).astype(LOW)
    far, near = to_far(own), to_near(own)
    shares = jnp.stack([features_back(share_one), features_back(share_two)]).reshape(-1, WINDOW)
    every_share = to_all(after_that(shares, own), ("seq", "ch"))
    (grad_mlp_gate_w,) = reduce_gate.sums()
    (grad_mlp_up_w,) = reduce_up.sums()
    far = meet(after_that(far, (grad_mlp_gate_w, grad_mlp_up_w)), reduce_branch)
    sent = reduce_branch.step()
    late_maps = after_that(maps, (sent, far))
    token_grad = assemble(cotangent, [own, far, near, to_near(far)], late_maps)
    result_pieces = [
        result_delta, result_far, result_near, to_near(after_that(result_far, beyond)),
    ]
    late_maps = after_that(maps, token_grad)
    result = assemble(tokens, result_pieces, late_maps)
    result = meet(result, reduce_branch)
    reduce_branch.step()
    every, every_share = after_that((every, every_share), result)
    every = every.astype(F32)
    grad_out_w, grad_gate_w, grad_in_w = reduce_branch.sums()
    norm_shares = jnp.sum(every_share, axis=0).reshape(2, width)
    every = every.reshape(-1, WINDOW)
    size = channels // blocks
    gate_w = every[: 2 * channels].reshape(2 * blocks, size, WINDOW)[:, :, :size]
    sums = every[2 * channels : 2 * channels + sum_rows.shape[0]].reshape(sums.shape)
    swapped = turn // 2 + turn % 2 * 2
    block_states = jnp.concatenate(
        [
            lax.dynamic_slice_in_dim(state[:, -1:, :], swapped ^ row, 1, axis=0)
            for row in ROW_ORDER
        ],
        axis=0,
    )
    return (
        result,
        block_states,
        token_grad,
        norm_shares[0],
        grad_gate_w,
        grad_in_w,
        grad_out_w.T,
        sums[1:5],
        sums[0],
        8.0 * jax.nn.sigmoid(-decay_param) * sums[5],
        gate_w[:blocks],
        sums[6],
        gate_w[blocks:],
        sums[7],
        norm_shares[1],
        grad_mlp_gate_w,
        grad_mlp_up_w,
        grad_down.T,
    )


def solution(mesh):
    in_specs = (
        P(None, "seq", None),
        P(None, "seq", None),
        P(),
        P(),
        P("seq", "ch"),
        P("seq", "ch"),
        P("ch", "seq"),
        P(None, "ch"),
        P("ch"),
        P("ch"),
        P("ch", None, None),
        P("ch"),
        P("ch", None, None),
        P("ch"),
        P(),
        P("seq", "ch"),
        P("seq", "ch"),
        P("ch", "seq"),
    )
    out_specs = (
        P(None, "seq", None),
        P(None, "seq", "ch"),
        P(None, "seq", None),
        P(),
        P("seq", "ch"),
        P("seq", "ch"),
        P("ch", "seq"),
        P(None, "ch"),
        P("ch"),
        P("ch"),
        P("ch", None, None),
        P("ch"),
        P("ch", None, None),
        P("ch"),
        P(),
        P("seq", "ch"),
        P("seq", "ch"),
        P("ch", "seq"),
    )
    return jax.shard_map(body, mesh=mesh, in_specs=in_specs, out_specs=out_specs, check_vma=False)
```

```python
import jax
import jax.numpy as jnp
from jax import lax
from jax.experimental import pallas as pl
from jax.experimental.pallas import tpu as pltpu
from jax.sharding import PartitionSpec as P

LOW = jnp.bfloat16
F32 = jnp.float32
EPS = 1e-06
GELU_A = 0.7978845608028654
GELU_B = 0.044715
VMEM_LIMIT = 48 * 1024 * 1024
RING_LIMIT = 8
WINDOW = 256
SMALL_COST = pl.CostEstimate(flops=1, bytes_accessed=1, transcendentals=0)


def ring_order(count):
    return list(range(0, count, 2)) + list(range(count - 1, 0, -2))


def ring_place(seq_index, count):
    return jnp.where(seq_index % 2 == 0, seq_index // 2, count - 1 - seq_index // 2)


def ring_member(place, count):
    place = place % count
    return jnp.where(place < count // 2, 2 * place, 2 * (count - 1 - place) + 1)


def ring_pairs(count):
    order = ring_order(count)
    ahead = [(order[i], order[(i + 1) % count]) for i in range(count)]
    behind = [(target, source) for source, target in ahead]
    return ahead, behind


def ring_blocks(count):
    if count > RING_LIMIT:
        return [jnp.int32(0)]
    here = ring_place(lax.axis_index("seq"), count)
    offsets = [0]
    for step in range(1, count // 2):
        offsets += [-step, step]
    return [ring_member(here + offset, count) for offset in offsets + [count // 2]]


def ring_block(offset, count):
    if abs(offset) == count // 2:
        return count - 1
    return 2 * offset if offset >= 0 else -2 * offset - 1


def after_that(value, others):
    return lax.optimization_barrier((value, others))[0]


def meet(value, *rings):
    value, pieces = lax.optimization_barrier((value, [ring.latest for ring in rings]))
    for ring, came in zip(rings, pieces, strict=True):
        ring.replace(came)
    return value


class Gather:
    def __init__(self, shards, others=()):
        self.count = lax.axis_size("seq")
        self.shards = shards
        joined = jnp.concatenate(shards, axis=1) if len(shards) > 1 else shards[0]
        self.latest, self.others = (joined, joined), others
        self.up, self.down = [self.latest[0]], [self.latest[1]]

    def replace(self, pieces):
        self.latest = pieces
        if self.count <= RING_LIMIT:
            self.up[-1], self.down[-1] = pieces

    def step(self):
        if self.count <= RING_LIMIT and len(self.up) <= self.count // 2:
            ahead, behind = ring_pairs(self.count)
            cut = self.shards[0].shape[0] // 2
            first, second = self.latest
            if len(self.up) == self.count // 2:
                first, second = first[:cut], second[cut:]
            first, second = after_that((first, second), self.others)
            self.others = ()
            self.up.append(lax.ppermute(first, "seq", ahead))
            self.down.append(lax.ppermute(second, "seq", behind))
            self.latest = (self.up[-1], self.down[-1])
        return self.latest

    def full(self):
        if self.count > RING_LIMIT:
            return [lax.all_gather(shard, "seq", axis=0, tiled=True) for shard in self.shards]
        pieces = [self.up[0]]
        for first, second in zip(self.up[1:], self.down[1:], strict=True):
            pieces += [first, second]
        full, start = [], 0
        for shard in self.shards:
            stop = start + shard.shape[1]
            full.append(jnp.concatenate([piece[:, start:stop] for piece in pieces], axis=0))
            start = stop
        return full


class Reduce:
    def __init__(self, fulls, others=()):
        self.count = lax.axis_size("seq")
        self.fulls = fulls
        self.left = self.count // 2
        self.latest, self.sent = (), ()
        self.others = others

    def replace(self, pieces):
        self.latest = pieces

    def step(self):
        if self.count <= RING_LIMIT and self.left > 0:
            ahead, behind = ring_pairs(self.count)
            up, down = ring_step(self.fulls, self.latest, self.count, self.left)
            up, down = after_that((up, down), self.others)
            self.others = ()
            self.sent = (up, down)
            self.latest = (lax.ppermute(up, "seq", ahead), lax.ppermute(down, "seq", behind))
            self.left -= 1
        return self.sent

    def sums(self):
        if self.count > RING_LIMIT:
            return [
                lax.psum_scatter(full.astype(F32), "seq", scatter_dimension=0, tiled=True)
                for full in self.fulls
            ]
        return ring_step(self.fulls, self.latest, self.count, 0)


def ring_step(fulls, came, count, step):
    half, rows = count // 2, fulls[0].shape[0] // count
    widths = [full.shape[1] for full in fulls]
    total = sum(widths)
    parts = 2
    piece = rows // parts
    first, last = step == half, step == 0

    def kernel(*refs):
        ups, downs = refs[: len(fulls)], refs[len(fulls) : 2 * len(fulls)]
        rest = refs[2 * len(fulls) :]
        got, out = rest[: len(came)], rest[len(came) :]
        place = pl.program_id(0)
        start = 0
        for index, width in enumerate(widths):
            columns = slice(start, start + width)
            start += width
            up, down = ups[index][...].astype(F32), downs[index][...].astype(F32)
            if last:
                out[index][...] = up + got[0][:, columns].astype(F32) + got[1][:, columns].astype(F32)
                continue
            if not first:
                plus, minus = got[0][:, columns].astype(F32), got[1][:, columns].astype(F32)
                if step == half - 1:
                    plus = jnp.where(place < parts // 2, plus, 0.0)
                    minus = jnp.where(place >= parts // 2, minus, 0.0)
                up, down = up + plus, down + minus
            out[0][:, columns] = up.astype(LOW)
            out[1][:, columns] = down.astype(LOW)

    def at(place, offset=0):
        block = ring_block(place, count)
        return lambda i: (block * parts + i + offset, 0)

    grid = parts // 2 if first else parts
    blocks = [pl.BlockSpec((piece, w), at(step)) for w in widths]
    blocks += [pl.BlockSpec((piece, w), at(-step, parts // 2 if first else 0)) for w in widths]
    got_specs = [pl.BlockSpec((piece, total), lambda i: (i, 0))] * len(came)
    if step == half - 1:
        got_specs = [
            pl.BlockSpec((piece, total), lambda i: (jnp.minimum(i, parts // 2 - 1), 0)),
            pl.BlockSpec((piece, total), lambda i: (jnp.maximum(i - parts // 2, 0), 0)),
        ]
    if last:
        out_specs = [pl.BlockSpec((piece, w), lambda i: (i, 0)) for w in widths]
        out_shape = [shape_of((rows, w)) for w in widths]
    else:
        out_specs = [pl.BlockSpec((piece, total), lambda i: (i, 0))] * 2
        out_shape = [shape_of((grid * piece, total), LOW)] * 2
    return pl.pallas_call(
        kernel, grid=(grid,), in_specs=blocks + got_specs, out_specs=out_specs,
        out_shape=out_shape, compiler_params=params(), cost_estimate=SMALL_COST, name="ring_step",
    )(*fulls, *fulls, *came)


ROW_ORDER = (0, 2, 1, 3)


def near_pairs(count):
    return [(c, c ^ 1) for c in range(count)]


def far_pairs(count):
    return [(c, c ^ 2) for c in range(count)]


def to_near(value):
    return lax.ppermute(value, "ch", near_pairs(lax.axis_size("ch")))


def to_far(value):
    return lax.ppermute(value, "ch", far_pairs(lax.axis_size("ch")))


def spread_rows(own):
    far, near = to_far(own), to_near(own)
    return [own, far, near, to_near(far)]


def sum_over(value, axis, dtype=F32):
    count, step = lax.axis_size(axis), 1
    while step < count:
        sent = value.astype(dtype)
        came = lax.ppermute(sent, axis, [(c, c ^ step) for c in range(count)])
        value = sent.astype(F32) + came.astype(F32)
        step *= 2
    return value


def carried(ends, backward):
    count, mine = lax.axis_size("seq"), lax.axis_index("seq")
    pieces = to_all(ends[:, :2].reshape(-1, ends.shape[2]), "seq").reshape(
        count, ends.shape[0], 2, ends.shape[2]
    )
    total = jnp.zeros_like(ends[:, 0])
    for place in range(count - 1):
        member = count - 1 - place if backward else place
        counts = member > mine if backward else member < mine
        piece = pieces[member]
        total = jnp.where(counts, piece[:, 0] * total + piece[:, 1], total)
    return total


def to_all(value, axis):
    count = lax.axis_size(axis)
    return lax.all_to_all(
        jnp.broadcast_to(value[None], (count,) + value.shape), axis, 0, 0, tiled=True
    )


def row_block(shape, column=0):
    return pl.BlockSpec((1,) + shape, lambda row, *_: (row, 0, column))


def whole_block(shape):
    return pl.BlockSpec(shape, lambda row, *_: (0,) * len(shape))


def gelu_parts(value):
    tanh = jnp.tanh(GELU_A * (value + GELU_B * value * value * value))
    act = 0.5 * value * (1.0 + tanh)
    slope = 0.5 * (1.0 + tanh) + 0.5 * value * (1.0 - tanh * tanh) * GELU_A * (
        1.0 + 3.0 * GELU_B * value * value
    )
    return act, slope


def gelu(value):
    return gelu_parts(value)[0]


def minus_expm1(value):
    series = jnp.full_like(value, 1.0 / 11.0)
    for divisor in range(10, 1, -1):
        series = (1.0 + value * series) * (1.0 / divisor)
    series = -value * (1.0 + value * series)
    return jnp.where(value > -0.8, series, 1.0 - jnp.exp(value))


def split(value):
    high = value.astype(LOW)
    return high, (value - high.astype(F32)).astype(LOW)


def dot(left, right, contract):
    return lax.dot_general(left, right, (contract, ((), ())), preferred_element_type=F32)


def dot_three(left, right, contract):
    (left_high, left_low), (right_high, right_low) = left, right
    return (
        dot(left_high, right_high, contract)
        + dot(left_high, right_low, contract)
        + dot(left_low, right_high, contract)
    )


def windows(count, size):
    starts = [min(block * size // 128 * 128, count * size - WINDOW) for block in range(count)]
    return [(start, block * size - start) for block, start in enumerate(starts)]


def window_dots(value, high_ref, low_ref, first, spots, contract):
    parts = []
    for index, (start, _) in enumerate(spots):
        piece = split(value[:, start : start + WINDOW])
        weight = (high_ref[first + index], low_ref[first + index])
        parts.append((start, dot_three(piece, weight, contract)))
    columns = []
    for tile in range(0, value.shape[1], 128):
        total = None
        for start, part in parts:
            if start <= tile < start + WINDOW:
                share = part[:, tile - start : tile - start + 128]
                total = share if total is None else total + share
        columns.append(total)
    return jnp.concatenate(columns, axis=1)


def decay_and_factor(recur, coef, reset):
    log_decay = coef * recur
    plain = jnp.exp(log_decay)
    decay = jnp.where(reset, 0.0, plain)
    factor = jnp.where(reset, 1.0, jnp.sqrt(minus_expm1(2.0 * log_decay)))
    return plain, decay, factor


def tile_scan(alpha, beta, backward):
    place = lax.broadcasted_iota(jnp.int32, alpha.shape, 1)
    for step in (1, 2, 4):
        turn = 8 - step if backward else step
        inside = place < 8 - step if backward else place >= step
        other_alpha = pltpu.roll(alpha, turn, 1)
        other_beta = pltpu.roll(beta, turn, 1)
        beta = jnp.where(inside, alpha * other_beta + beta, beta)
        alpha = jnp.where(inside, alpha * other_alpha, alpha)
    return alpha, beta


def join_tiles(alpha_ref, beta_ref, backward):
    length, channels = alpha_ref.shape[1], alpha_ref.shape[2]
    groups = length // 8

    def step(index, carry):
        alpha_carry, beta_carry = carry
        group = groups - 1 - index if backward else index
        rows = pl.ds(pl.multiple_of(group * 8, 8), 8)
        alpha, beta = alpha_ref[0, rows, :], beta_ref[0, rows, :]
        beta = alpha * beta_carry + beta
        alpha = alpha * alpha_carry
        alpha_ref[0, rows, :] = alpha
        beta_ref[0, rows, :] = beta
        last = 0 if backward else 7
        return alpha[last : last + 1], beta[last : last + 1]

    start = (jnp.ones((1, channels), F32), jnp.zeros((1, channels), F32))
    return lax.fori_loop(0, groups, step, start, unroll=4)


def forward_kernel(
    input_ref, halo_ref, mask_ref, taps_ref, bias_ref, coef_ref, high_ref, low_ref, gate_bias_ref,
    conv_ref, recur_ref, gate_ref, alpha_ref, beta_ref, export_ref, extended,
):
    length, channels = input_ref.shape[1], input_ref.shape[2]
    extended[0:8, :] = halo_ref[0]
    extended[8 : 8 + length, :] = input_ref[0]
    masks = mask_ref[0]
    conv = bias_ref[...] + taps_ref[0:1, :] * input_ref[0]
    for lag in (1, 2, 3):
        lagged = extended[8 - lag : 8 - lag + length, :]
        conv = conv + taps_ref[lag : lag + 1, :] * lagged * masks[:, lag : lag + 1]
    conv_ref[0] = conv
    count = high_ref.shape[0] // 2
    spots = windows(count, channels // count)
    before = [
        window_dots(conv, high_ref, low_ref, first, spots, ((1,), (0,))) for first in (0, count)
    ]
    recur = jax.nn.sigmoid(before[0] + gate_bias_ref[:, :channels])
    gate = jax.nn.sigmoid(before[1] + gate_bias_ref[:, channels:])
    recur_ref[0] = recur
    gate_ref[0] = gate
    reset = masks[:, 0:1] > 0.5
    _, decay, factor = decay_and_factor(recur, coef_ref[...], reset)
    driven = factor * gate * conv
    grouped = (length // 8, 8, channels)
    alpha, beta = tile_scan(decay.reshape(grouped), driven.reshape(grouped), False)
    alpha_ref[0] = alpha.reshape(length, channels)
    beta_ref[0] = beta.reshape(length, channels)
    alpha, beta = join_tiles(alpha_ref, beta_ref, False)
    export_ref[0] = jnp.concatenate([alpha, beta, jnp.zeros((6, channels), F32)], axis=0)


def backscan_kernel(
    mixed_ref, pre_ref, state_ref, recur_ref, mask_ref, coef_ref,
    pre_grad_ref, alpha_ref, beta_ref, export_ref, extended,
):
    length, channels = mixed_ref.shape[1], mixed_ref.shape[2]
    act, slope = gelu_parts(pre_ref[0])
    mixed = mixed_ref[0]
    pre_grad_ref[0] = (mixed * state_ref[0] * slope).astype(LOW)
    reset = mask_ref[0][:, 0:1] > 0.5
    decay = jnp.where(reset, 0.0, jnp.exp(coef_ref[...] * recur_ref[0]))
    extended[0:length, :] = decay
    extended[length : length + 8, :] = jnp.ones((8, channels), F32)
    following = extended[1 : 1 + length, :]
    grouped = (length // 8, 8, channels)
    alpha, beta = tile_scan(following.reshape(grouped), (mixed * act).reshape(grouped), True)
    alpha_ref[0] = alpha.reshape(length, channels)
    beta_ref[0] = beta.reshape(length, channels)
    alpha, beta = join_tiles(alpha_ref, beta_ref, True)
    first = extended[0:1, :]
    export_ref[0] = jnp.concatenate(
        [first * alpha, first * beta, jnp.zeros((6, channels), F32)], axis=0
    )


def backward_kernel(
    alpha_ref, beta_ref, incoming_ref, state_ref, carry_ref, recur_ref, gate_ref, conv_ref,
    input_ref, halo_ref, mask_ref, taps_ref, coef_ref, high_ref, low_ref, pre_grad_ref,
    grad_ref, tail_ref, head_ref, weight_ref, sums_ref, extended, masked, weight_acc,
):
    length, channels = alpha_ref.shape[1], alpha_ref.shape[2]

    @pl.when(pl.program_id(0) == 0)
    def _():
        weight_acc[...] = jnp.zeros_like(weight_acc)
        sums_ref[...] = jnp.zeros_like(sums_ref)

    masks = mask_ref[0]
    reset = masks[:, 0:1] > 0.5
    recur, gate, conv, coef = recur_ref[0], gate_ref[0], conv_ref[0], coef_ref[...]
    plain, decay, factor = decay_and_factor(recur, coef, reset)
    grad = beta_ref[0] + alpha_ref[0] * incoming_ref[0]
    extended[0:8, :] = jnp.broadcast_to(carry_ref[0], (8, channels))
    extended[8 : 8 + length, :] = state_ref[0]
    prior = extended[7 : 7 + length, :]
    grad_decay = grad * prior
    grad_factor = grad * gate * conv
    grad_log = jnp.where(reset, 0.0, grad_decay * decay - grad_factor * plain * plain / factor)
    grad_recur = coef * grad_log * recur * (1.0 - recur)
    grad_gate = grad * factor * conv * gate * (1.0 - gate)
    count = high_ref.shape[0] // 2
    size = channels // count
    spots = windows(count, size)
    grad_conv = grad * factor * gate
    for first, values in ((0, grad_recur), (count, grad_gate)):
        for index, (start, _) in enumerate(spots):
            columns = slice(start, start + WINDOW)
            pair = split(conv[:, columns]), split(values[:, columns])
            weight_acc[first + index] += dot_three(*pair, ((0,), (0,)))
        grad_conv = grad_conv + window_dots(
            values, high_ref, low_ref, first, spots, ((1,), (1,))
        )

    @pl.when(pl.program_id(0) == pl.num_programs(0) - 1)
    def _():
        for index in range(2 * count):
            place = spots[index % count][1]
            turned = weight_acc[index]
            if place:
                turned = pltpu.roll(turned, WINDOW - place, 1)
            weight_ref[index] = turned[place : place + size].astype(LOW)


    def total(value):
        return jnp.sum(value, axis=0, keepdims=True)

    extended[0:8, :] = halo_ref[0]
    extended[8 : 8 + length, :] = input_ref[0]
    sums = [total(grad_conv), total(grad_conv * input_ref[0])]
    masked[0:8, :] = jnp.zeros((8, channels), F32)
    masked[8 + length : 16 + length, :] = jnp.zeros((8, channels), F32)
    spread = taps_ref[0:1, :] * grad_conv
    head = jnp.zeros((8, channels), F32)
    for lag in (1, 2, 3):
        kept = grad_conv * masks[:, lag : lag + 1]
        sums.append(total(kept * extended[8 - lag : 8 - lag + length, :]))
        masked[8 : 8 + length, :] = kept
        tap = taps_ref[lag : lag + 1, :]
        spread = spread + tap * masked[8 + lag : 8 + lag + length, :]
        head = head + tap * masked[lag : 8 + lag, :]
    sums += [total(recur * grad_log), total(grad_recur), total(grad_gate)]
    sums_ref[...] += jnp.concatenate(sums, axis=0)
    grad_ref[0, :, :channels] = spread.astype(LOW)
    grad_ref[0, :, channels:] = pre_grad_ref[0]
    tail_ref[0] = spread[length - 8 :, :]
    head_ref[0] = head


def params():
    return pltpu.CompilerParams(
        dimension_semantics=("arbitrary",), vmem_limit_bytes=VMEM_LIMIT
    )


def shape_of(shape, dtype=F32):
    return jax.ShapeDtypeStruct(shape, dtype)


def run_forward(pre, halo, masks, taps, bias, coef, high, low, gate_bias):
    rows, length, channels = pre.shape[0], pre.shape[1], taps.shape[1]
    block = row_block((length, channels))
    return pl.pallas_call(
        forward_kernel,
        grid=(rows,),
        in_specs=[
            block, row_block((8, channels)), row_block((length, 8)), whole_block((4, channels)),
            whole_block((1, channels)), whole_block((1, channels)), whole_block(high.shape),
            whole_block(low.shape), whole_block((1, 2 * channels)),
        ],
        out_specs=[block] * 5 + [row_block((8, channels))],
        out_shape=[shape_of((rows, length, channels))] * 5 + [shape_of((rows, 8, channels))],
        scratch_shapes=[pltpu.VMEM((length + 8, channels), F32)],
        compiler_params=params(), cost_estimate=SMALL_COST,
        name="forward_scan",
    )(pre, halo, masks, taps, bias, coef, high, low, gate_bias)


def run_backscan(mixed, pre, state, recur, masks, coef):
    rows, length, channels = mixed.shape
    block = row_block((length, channels))
    return pl.pallas_call(
        backscan_kernel,
        grid=(rows,),
        in_specs=[
            block, row_block((length, channels), 1), block, block, row_block((length, 8)),
            whole_block((1, channels)),
        ],
        out_specs=[block] * 3 + [row_block((8, channels))],
        out_shape=[
            shape_of(mixed.shape, LOW), shape_of(mixed.shape), shape_of(mixed.shape),
            shape_of((rows, 8, channels)),
        ],
        scratch_shapes=[pltpu.VMEM((length + 8, channels), F32)],
        compiler_params=params(), cost_estimate=SMALL_COST,
        name="backward_scan",
    )(mixed, pre, state, recur, masks, coef)


def run_backward(
    alpha, beta, incoming, state, carry, recur, gate, conv, pre, halo, masks, taps, coef, high, low, pre_grad
):
    rows, length, channels = alpha.shape
    block, edge, line = (
        row_block((length, channels)), row_block((8, channels)), row_block((1, channels)),
    )
    weights = (high.shape[0], 2 * channels // high.shape[0], WINDOW)
    return pl.pallas_call(
        backward_kernel,
        grid=(rows,),
        in_specs=[
            block, block, line, block, line, block, block, block, block, edge,
            row_block((length, 8)), whole_block((4, channels)), whole_block((1, channels)),
            whole_block(high.shape), whole_block(low.shape), block,
        ],
        out_specs=[row_block((length, 2 * channels)), edge, edge, whole_block(weights), whole_block((8, channels))],
        out_shape=[
            shape_of((rows, length, 2 * channels), LOW), shape_of((rows, 8, channels)),
            shape_of((rows, 8, channels)), shape_of(weights, LOW), shape_of((8, channels)),
        ],
        scratch_shapes=[
            pltpu.VMEM((length + 8, channels), F32), pltpu.VMEM((length + 16, channels), F32),
            pltpu.VMEM(high.shape, F32),
        ],
        compiler_params=params(), cost_estimate=SMALL_COST,
        name="branch_backward",
    )(alpha, beta, incoming, state, carry, recur, gate, conv, pre, halo, masks, taps, coef, high, low, pre_grad)


def back_project(lefts, rights):
    rows, length, _ = lefts[0].shape
    width, tile = rights[0].shape[0], 256
    half = rows // 2

    def kernel(*refs):
        total = None
        for left, right in zip(refs[: len(lefts)], refs[len(lefts) : 2 * len(lefts)], strict=True):
            flat = left[...].reshape(rows * length, left.shape[2])
            share = dot(flat, right[...], ((1,), (1,)))
            total = share if total is None else total + share
        total = total.reshape(rows, length, tile)
        refs[-2][...] = total[:half]
        refs[-1][...] = total[half:].astype(LOW)

    out = pl.BlockSpec((half, length, tile), lambda i: (0, 0, i))
    in_specs = [pl.BlockSpec(left.shape, lambda i: (0, 0, 0)) for left in lefts]
    in_specs += [pl.BlockSpec((tile, right.shape[1]), lambda i: (i, 0)) for right in rights]
    return pl.pallas_call(
        kernel, grid=(width // tile,), in_specs=in_specs, out_specs=[out, out],
        out_shape=[shape_of((half, length, width)), shape_of((half, length, width), LOW)],
        compiler_params=params(), cost_estimate=SMALL_COST, name="back_project",
    )(*lefts, *rights)


def joined(kept, came):
    total = kept + came.astype(F32)
    return total[0:1], total[1:2].astype(LOW)


def part(index, width):
    return pl.ds(pl.multiple_of(index * width, 128), width)


def norm_kernel(row_map, block_map, gain_ref, values_ref, out_ref):
    blocks = block_map.shape[0]
    width = values_ref.shape[2] // blocks
    values = values_ref[0]
    root = lax.rsqrt(jnp.mean(values * values, axis=-1, keepdims=True) + EPS)
    for place in range(blocks):
        there = part(block_map[place], width)
        normed = values_ref[0, :, there] * root * gain_ref[:, there]
        out_ref[0, :, place * width : (place + 1) * width] = normed.astype(LOW)


def relative_kernel(row_map, block_map, values_ref, own_ref, *out_refs):
    blocks = block_map.shape[0]
    width = values_ref.shape[2] // blocks
    for place in range(blocks):
        there = part(block_map[place], width)
        here = slice(place * width, (place + 1) * width)
        for out_ref in out_refs:
            out_ref[0, :, here] = values_ref[0, :, there].astype(LOW)

        @pl.when(pl.program_id(0) == 0)
        def _():
            own_ref[0, :, here] = values_ref[0, :, there]


def assemble_kernel(row_map, block_map, base_ref, *refs):
    pieces, out_ref = refs[:-1], refs[-1]
    blocks = block_map.shape[0]
    width = base_ref.shape[2] // blocks
    for row, piece in enumerate(pieces):

        @pl.when(pl.program_id(0) == row)
        def _():
            for place in range(blocks):
                there = part(block_map[place], width)
                here = slice(place * width, (place + 1) * width)
                out_ref[0, :, there] = base_ref[0, :, there] + piece[0, :, here].astype(F32)


def arranged(kernel, maps, out_shape, in_specs, out_specs, *arrays):
    return pl.pallas_call(
        kernel,
        grid_spec=pltpu.PrefetchScalarGridSpec(
            num_scalar_prefetch=2, grid=(maps[0].shape[0],), in_specs=in_specs, out_specs=out_specs
        ),
        out_shape=out_shape,
        compiler_params=params(), cost_estimate=SMALL_COST,
    )(*maps, *arrays)


def mapped_row(shape):
    return pl.BlockSpec((1,) + shape, lambda row, row_map, block_map: (row_map[row], 0, 0))


def relative_norm(values, gain, maps):
    shape = values.shape[1:]
    return arranged(
        norm_kernel, maps, shape_of(values.shape, LOW),
        [whole_block((1, shape[1])), mapped_row(shape)], row_block(shape), gain[None, :], values,
    )


def relative_rows(values, maps, rounded):
    shape = values.shape[1:]
    shapes, specs = [shape_of((1,) + shape)], [whole_block((1,) + shape)]
    if rounded:
        shapes, specs = shapes + [shape_of(values.shape, LOW)], specs + [row_block(shape)]
    if not rounded:
        maps = (maps[0][:1], maps[1])
    return arranged(relative_kernel, maps, shapes, [mapped_row(shape)], specs, values)


def assemble(base, pieces, maps):
    shape = base.shape[1:]
    return arranged(
        assemble_kernel, maps, shape_of(base.shape),
        [mapped_row(shape)] + [whole_block((1,) + shape)] * len(pieces), mapped_row(shape),
        base, *pieces,
    )


def project(left, right):
    return jnp.einsum("rtd,df->rtf", left, right, preferred_element_type=F32)


def project_back(left, right):
    return jnp.einsum("rtf,df->rtd", left, right, preferred_element_type=F32)


def outer_sum(left, right):
    return jnp.einsum("rtd,rtf->df", left, right, preferred_element_type=F32).astype(LOW)


def inverse_root(values):
    return lax.rsqrt(jnp.mean(values * values, axis=-1, keepdims=True) + EPS)


def norm_back(grad, values, root, gain):
    scaled = grad * gain
    inner = jnp.mean(scaled * values, axis=-1, keepdims=True)
    share = jnp.sum(grad * values * root, axis=(0, 1))
    return root * scaled - values * (root * root * root) * inner, share


def gate_matrix_kernel(recur_ref, input_ref, high_ref, low_ref):
    count, size = recur_ref.shape[0], recur_ref.shape[1]
    high_ref[...] = jnp.zeros_like(high_ref)
    low_ref[...] = jnp.zeros_like(low_ref)
    for index, ref in enumerate((recur_ref, input_ref)):
        for block, (_, place) in enumerate(windows(count, size)):
            high, low = split(ref[block])
            here = slice(place, place + size)
            high_ref[index * count + block, here, here] = high
            low_ref[index * count + block, here, here] = low


def gate_matrix(recur_weight, input_weight):
    shape = shape_of((2 * recur_weight.shape[0], WINDOW, WINDOW), LOW)
    return pl.pallas_call(
        gate_matrix_kernel, out_shape=[shape, shape],
        compiler_params=pltpu.CompilerParams(vmem_limit_bytes=VMEM_LIMIT), cost_estimate=SMALL_COST, name="gate_matrix",
    )(recur_weight, input_weight)


def body(
    tokens, cotangent, doc_starts, norm1_gain, branch_gate_w, branch_in_w, branch_out_w,
    conv_weight, conv_bias, decay_param, recur_gate_w, recur_gate_b, input_gate_w, input_gate_b,
    norm2_gain, mlp_gate_w, mlp_up_w, mlp_down_w,
):
    rows, length, width = tokens.shape
    channels, blocks = conv_bias.shape[0], recur_gate_w.shape[0]
    seq_count = lax.axis_size("seq")
    mine, turn = lax.axis_index("seq"), lax.axis_index("ch")
    row_map = jnp.stack([turn ^ row for row in ROW_ORDER]).astype(jnp.int32)
    block_map = jnp.stack(ring_blocks(seq_count)).astype(jnp.int32)
    maps = (row_map, block_map)

    def row_of(values, row):
        return lax.dynamic_slice_in_dim(values, turn ^ ROW_ORDER[row], 1, axis=0)

    def features(values):
        return jnp.take(values.reshape(block_map.shape[0], -1), block_map, axis=0).reshape(-1)

    def features_back(values):
        there = jnp.argmax(block_map[None, :] == jnp.arange(block_map.shape[0])[:, None], axis=1)
        return jnp.take(values.reshape(block_map.shape[0], -1), there, axis=0).reshape(-1)

    gather_one = Gather(
        [
            jnp.concatenate([branch_in_w.astype(LOW), branch_gate_w.astype(LOW)], axis=1),
            branch_out_w.astype(LOW).T,
        ]
    )
    came = gather_one.step()

    starts = jnp.concatenate([row_of(doc_starts, j) for j in range(rows)], axis=0)
    positions = mine * length - 3 + jnp.arange(length + 3, dtype=jnp.int32)
    reset_ext = jnp.any(starts[:, :, None] == positions[None, None, :], axis=1)
    blocked = reset_ext[:, 3:]
    columns = [blocked.astype(F32)]
    for lag in (1, 2, 3):
        columns.append(jnp.where(blocked, 0.0, 1.0))
        blocked = blocked | reset_ext[:, 3 - lag : 3 - lag + length]
    masks = jnp.stack(columns + [jnp.zeros_like(columns[0])] * 4, axis=-1)

    gate_bias = jnp.concatenate([recur_gate_b, input_gate_b])[None, :]
    coef = (-8.0 * jax.nn.softplus(-decay_param))[None, :]
    gain_one, gain_two = features(norm1_gain), features(norm2_gain)
    mlp_shards = [mlp_gate_w.astype(LOW), mlp_up_w.astype(LOW)]
    down_shards = [mlp_down_w.astype(LOW).T]

    before = after_that(tokens[:, -8:, :], came)
    before = lax.ppermute(before, "seq", [(s, s + 1) for s in range(seq_count - 1)])
    first_maps = after_that(maps, (came, masks))
    came = gather_one.step()
    hidden_one = relative_norm(tokens, norm1_gain, first_maps)
    hidden_before = relative_norm(before, norm1_gain, first_maps)
    recur_weights = after_that(recur_gate_w, (came, hidden_one))
    came = gather_one.step()
    high, low = gate_matrix(recur_weights, input_gate_w)
    gather_two = Gather(mlp_shards, gather_one.step())
    gather_two.step()
    in_gate, output_full = gather_one.full()

    pre = project(hidden_one, in_gate)
    halo = project(hidden_before, in_gate)
    conv, recur, gate, decay_sum, state_part, export = run_forward(
        pre, halo, masks, conv_weight, conv_bias[None, :], coef, high, low, gate_bias
    )
    export = meet(export, gather_two)
    carry = carried(export, False)[:, None, :]
    came = gather_two.step()
    state = state_part + decay_sum * carry
    mixed = (gelu(pre[:, :, channels:]) * state).astype(LOW)

    kept, away = back_project([mixed], [output_full])
    kept, beyond = joined(kept, to_near(away))
    arrived = to_far(beyond)
    late_maps = after_that(maps, beyond)
    (tokens_own,) = relative_rows(tokens, late_maps, False)
    cotangent_own, grad_two = relative_rows(cotangent, late_maps, True)
    kept = meet(after_that(kept, (tokens_own, cotangent_own)), gather_two)
    after = tokens_own + (kept + arrived.astype(F32))
    came = gather_two.step()
    root_two = inverse_root(after)
    spread = spread_rows((after * root_two * gain_two).astype(LOW))
    gather_three = Gather(down_shards, gather_two.step())
    came = gather_three.step()
    hidden_two = jnp.concatenate(spread, axis=0)
    mlp_gate_full, mlp_up_full = gather_two.full()
    pre_mlp = project(hidden_two, mlp_gate_full)
    mlp_up_full = after_that(mlp_up_full, (came, pre_mlp))
    came = gather_three.step()
    pre_up = project(hidden_two, mlp_up_full)
    product = (gelu(pre_mlp) * pre_up).astype(LOW)
    grad_two = after_that(grad_two, (came, product))
    came = gather_three.step()
    down_part = outer_sum(grad_two, product)
    reduce_down = Reduce([down_part], gather_three.step())
    (mlp_down_full,) = gather_three.full()

    sent = reduce_down.step()
    grad_product = project(grad_two, after_that(mlp_down_full, sent))
    act, slope = gelu_parts(pre_mlp)
    grad_up = (grad_product * act).astype(LOW)
    grad_mlp = meet((grad_product * pre_up * slope).astype(LOW), reduce_down)
    sent = reduce_down.step()

    kept, away = back_project([after_that(grad_mlp, sent), grad_up], [mlp_gate_full, mlp_up_full])
    away = meet(away, reduce_down)
    sent = reduce_down.step()
    kept, beyond = joined(kept, after_that(to_near(away), sent))
    arrived = to_far(beyond)
    mlp_gate_part = outer_sum(after_that(hidden_two, beyond), grad_mlp)
    mlp_gate_part = meet(mlp_gate_part, reduce_down)
    sent = reduce_down.step()
    arrived = after_that(arrived, sent)
    back_two, share_two = norm_back(kept + arrived.astype(F32), after, root_two, gain_two)
    grad_after = cotangent_own + back_two
    own = grad_after.astype(LOW)
    far, near = to_far(own), to_near(own)
    mlp_up_part = outer_sum(after_that(hidden_two, own), grad_up)
    mlp_up_part = meet(mlp_up_part, reduce_down)
    reduce_gate = Reduce([mlp_gate_part], reduce_down.latest)
    sent = reduce_gate.step()
    result_kept, result_away = back_project(
        [after_that(product, (sent, mlp_up_part))], [mlp_down_full]
    )
    (grad_down,) = reduce_down.sums()
    result_away = meet(result_away, reduce_gate)
    reduce_up = Reduce([mlp_up_part], reduce_gate.latest)
    sent = (reduce_up.step(), reduce_gate.step())
    far = after_that(far, sent)
    result_came = to_near(after_that(result_away, far))
    grad_one = jnp.concatenate([own, far, near, to_near(far)], axis=0)

    grad_mixed = project(after_that(grad_one, sent), output_full)
    grad_pre_gate, tail_decay, grad_part, export = run_backscan(
        grad_mixed, pre, state, recur, masks, coef
    )
    export = meet(export, reduce_gate, reduce_up)
    incoming = carried(export, True)[:, None, :]
    reduce_gate.others = reduce_up.others = incoming
    sent = (reduce_up.step(), reduce_gate.step())
    grad_pre, tail, head, gate_grads, sums = run_backward(
        tail_decay, grad_part, incoming, state, carry, recur, gate, conv, pre, halo, masks,
        conv_weight, coef, high, low, grad_pre_gate,
    )
    head = meet(head, reduce_up)
    sent = reduce_up.step()
    result_kept, result_beyond = joined(result_kept, after_that(result_came, (head, sent)))
    result_arrived = to_far(result_beyond)
    beyond = lax.ppermute(head, "seq", [(s + 1, s) for s in range(seq_count - 1)])
    out_part = outer_sum(grad_one, after_that(mixed, result_beyond))
    beyond = after_that(beyond, out_part)
    grad_pre = lax.dynamic_update_slice(grad_pre, (tail + beyond).astype(LOW), (0, length - 8, 0))
    kept, away = back_project([grad_pre], [in_gate])
    away = meet(away, reduce_gate, reduce_up)
    reduce_gate.others = away
    sent = reduce_gate.step()
    came = to_near(away)
    gate_part = outer_sum(after_that(hidden_one, sent), grad_pre_gate)
    kept, beyond = joined(kept, after_that(came, gate_part))
    beyond = meet(beyond, reduce_gate)
    arrived = to_far(beyond)
    reduce_up.others = beyond
    sent = reduce_up.step()

    in_part = outer_sum(after_that(hidden_one, (sent, beyond)), grad_pre[:, :, :channels])
    sum_rows = sums.astype(LOW).reshape(-1, WINDOW)
    small = jnp.concatenate(
        [
            gate_grads.reshape(-1, WINDOW),
            jnp.pad(sum_rows, ((0, -sum_rows.shape[0] % seq_count), (0, 0))),
        ]
    )
    small = after_that(small.reshape(seq_count, -1, WINDOW), in_part)
    result_arrived = after_that(result_arrived, in_part)
    result_delta = (after + (result_kept + result_arrived.astype(F32)) - tokens_own).astype(LOW)
    result_far, result_near = to_far(result_delta), to_near(result_delta)
    in_part = after_that(in_part, (small, result_delta))
    small = lax.all_to_all(small, "seq", 0, 0, tiled=True)
    small = jnp.sum(small.astype(F32), axis=0).astype(LOW)
    every = to_all(small, "seq")
    in_part = meet(in_part, reduce_gate, reduce_up)
    reduce_branch = Reduce([out_part, gate_part, in_part], reduce_up.latest)
    sent = reduce_branch.step()

    arrived = after_that(arrived, sent)
    back_one, share_one = norm_back(
        kept + arrived.astype(F32), tokens_own, inverse_root(tokens_own), gain_one
    )
    token_own = meet(grad_after + back_one, reduce_branch)
    sent = reduce_branch.step()
    own = (token_own - cotangent_own).astype(LOW)
    far, near = to_far(own), to_near(own)
    shares = jnp.stack([features_back(share_one), features_back(share_two)]).reshape(-1, WINDOW)
    every_share = to_all(after_that(shares, own), ("seq", "ch"))
    (grad_mlp_gate_w,) = reduce_gate.sums()
    (grad_mlp_up_w,) = reduce_up.sums()
    far = meet(after_that(far, (grad_mlp_gate_w, grad_mlp_up_w)), reduce_branch)
    sent = reduce_branch.step()
    late_maps = after_that(maps, (sent, far))
    token_grad = assemble(cotangent, [own, far, near, to_near(far)], late_maps)
    result_pieces = [
        result_delta, result_far, result_near, to_near(after_that(result_far, far)),
    ]
    late_maps = after_that(maps, token_grad)
    result = assemble(tokens, result_pieces, late_maps)
    result = meet(result, reduce_branch)
    reduce_branch.step()
    every, every_share = after_that((every, every_share), result)
    every = every.astype(F32)
    grad_out_w, grad_gate_w, grad_in_w = reduce_branch.sums()
    norm_shares = jnp.sum(every_share, axis=0).reshape(2, width)
    every = every.reshape(-1, WINDOW)
    size = channels // blocks
    gate_w = every[: 2 * channels].reshape(2 * blocks, size, WINDOW)[:, :, :size]
    sums = every[2 * channels : 2 * channels + sum_rows.shape[0]].reshape(sums.shape)
    swapped = turn // 2 + turn % 2 * 2
    block_states = jnp.concatenate(
        [
            lax.dynamic_slice_in_dim(state[:, -1:, :], swapped ^ row, 1, axis=0)
            for row in ROW_ORDER
        ],
        axis=0,
    )
    return (
        result,
        block_states,
        token_grad,
        norm_shares[0],
        grad_gate_w,
        grad_in_w,
        grad_out_w.T,
        sums[1:5],
        sums[0],
        8.0 * jax.nn.sigmoid(-decay_param) * sums[5],
        gate_w[:blocks],
        sums[6],
        gate_w[blocks:],
        sums[7],
        norm_shares[1],
        grad_mlp_gate_w,
        grad_mlp_up_w,
        grad_down.T,
    )


def solution(mesh):
    in_specs = (
        P(None, "seq", None),
        P(None, "seq", None),
        P(),
        P(),
        P("seq", "ch"),
        P("seq", "ch"),
        P("ch", "seq"),
        P(None, "ch"),
        P("ch"),
        P("ch"),
        P("ch", None, None),
        P("ch"),
        P("ch", None, None),
        P("ch"),
        P(),
        P("seq", "ch"),
        P("seq", "ch"),
        P("ch", "seq"),
    )
    out_specs = (
        P(None, "seq", None),
        P(None, "seq", "ch"),
        P(None, "seq", None),
        P(),
        P("seq", "ch"),
        P("seq", "ch"),
        P("ch", "seq"),
        P(None, "ch"),
        P("ch"),
        P("ch"),
        P("ch", None, None),
        P("ch"),
        P("ch", None, None),
        P("ch"),
        P(),
        P("seq", "ch"),
        P("seq", "ch"),
        P("ch", "seq"),
    )
    return jax.shard_map(body, mesh=mesh, in_specs=in_specs, out_specs=out_specs, check_vma=False)
```
